32 devices in a mesh: row: 4 (over z), col: 8 (over y, x, core).
Axes of the slice: x: 2, y: 2, z: 4, core: 2. Of those that a mesh axis runs over, the one named last changes fastest.
Arguments:
- factor: bfloat16 [16, 4, 8, 8, 128, 128], P(None, 'row', None, 'col'), may hold values from -0.09375 to 0.09375
- pattern: int32 [16, 4, 8, 8], P(None, 'row', None, 'col'), may hold values 0 or 1
- loads: float32 [8, 8, 128, 256], P(None, 'col'), may hold values from -6 to 6
- block_inverse: float32 [8, 8, 128, 128], P(None, 'col'), may hold values from -1 to 2, as said below
Outputs:
- solution: float32 [8, 8, 128, 256], P(None, 'col')
The draws below stay inside these ranges and needn't reach their ends.
Inputs may be any that keep to these rules, and one draw needn't show every extreme that they name: `block_inverse`: each block is lower triangular with diagonal entries between 0.5 and 1.5.
All inputs are finite; a program needn't handle non-finite values. No bound on the sum of `pattern` on one device may be relied on, other than what follows from the above.
Results may differ from the reference program's by a relative error of at most 0.0045.
Values may be sent and summed in bfloat16 or wider, within the bound.
A program may use at most 128 MiB of HBM per device.

```python
import math
import jax
import jax.numpy as jnp
from jax import lax

BLOCK = 128
SCENARIOS = 256
LEVELS = 8
COL_BLOCKS = 1
LEVEL_BLOCKS = 8
BLOCKS = 64
N_ROW = 4
N_COL = 8


def draw_block_inverse(key, part):
    key_off, key_diag = jax.random.split(key)
    rows = lax.broadcasted_iota(jnp.int32, (BLOCK, BLOCK), 0)
    cols = lax.broadcasted_iota(jnp.int32, (BLOCK, BLOCK), 1)
    lower = (cols < rows).astype(jnp.float32)
    unit = (cols == rows).astype(jnp.float32)
    off_part = jax.random.normal(key_off, (BLOCKS, BLOCK, BLOCK), jnp.float32) * (0.5 / math.sqrt(BLOCK))
    off_part = jnp.clip(off_part, -0.9, 0.9)
    diag_part = jax.random.uniform(key_diag, (BLOCKS, 1, BLOCK), jnp.float32, 0.5, 1.5)
    blocks = off_part * lower + diag_part * unit
    return blocks.reshape(BLOCKS // N_COL, N_COL, BLOCK, BLOCK)


def set_ends(values, rng, least, top_value):
    place = [jax.random.randint(jax.random.fold_in(rng, axis), (), 0, length) for axis, length in enumerate(values.shape)]
    widest = values.shape.index(max(values.shape))
    beside = place[:widest] + [(place[widest] + 1) % values.shape[widest]] + place[widest + 1:]
    return values.at[tuple(place)].set(least).at[tuple(beside)].set(top_value)


def levels(rng, shape, cuts, least, largest):
    level, own = 1.0, jax.random.fold_in(rng, 6)
    for position, blocks in cuts:
        steps = jnp.exp(jax.random.uniform(jax.random.fold_in(own, position), (blocks,), jnp.float32, least / len(cuts), largest / len(cuts)))
        level = level * jnp.repeat(steps, shape[position] // blocks).reshape([-1 if axis == position else 1 for axis in range(len(shape))])
    return level


def scatter_about(rng, dims, scale, most, pieces=(), kind=jnp.bfloat16):
    values = scale * jax.random.normal(rng, dims, jnp.float32)
    if pieces:
        values = values * levels(rng, dims, pieces, -0.22, 0.18)
    return jnp.clip(values, -most, most).astype(kind)


def setup_inputs(seed: int = 0) -> dict:
    arg_keys = jax.random.split(jax.random.key(seed), 5)
    factor = scatter_about(arg_keys[0], (BLOCKS // N_ROW, N_ROW, BLOCKS // N_COL, N_COL, BLOCK, BLOCK), (BLOCKS * BLOCK // 2) ** -0.5, 0.09375, ((1, 4), (3, 8)))
    pattern = set_ends((jax.random.randint(arg_keys[1], (BLOCKS // N_ROW, N_ROW, BLOCKS // N_COL, N_COL), 0, 2) < 1).astype(jnp.int32), jax.random.fold_in(arg_keys[1], 1), 0, 1)
    loads = scatter_about(arg_keys[2], (BLOCKS // N_COL, N_COL, BLOCK, SCENARIOS), 1.0, 6.0, ((1, 8),), jnp.float32)
    block_inverse = draw_block_inverse(jax.random.fold_in(arg_keys[4], 71), 0)
    return dict(factor=factor, pattern=pattern, loads=loads, block_inverse=block_inverse)


def reference(factor, pattern, loads, block_inverse):
    masked = factor * pattern.astype(jnp.bfloat16)[:, :, :, :, None, None]
    per_row = LEVEL_BLOCKS // N_ROW
    rhs_all = loads.reshape(BLOCKS, BLOCK, SCENARIOS)
    inverse_all = block_inverse.reshape(BLOCKS, BLOCK, BLOCK)
    forward_vals = []
    forward_low = []
    for level_id in range(LEVELS):
        start = level_id * LEVEL_BLOCKS
        rhs_level = rhs_all[start:start + LEVEL_BLOCKS]
        if level_id > 0:
            panel = masked[level_id * per_row:(level_id + 1) * per_row, :, :level_id * COL_BLOCKS, :]
            panel = panel.reshape(LEVEL_BLOCKS, level_id * LEVEL_BLOCKS, BLOCK, BLOCK)
            earlier = jnp.concatenate(forward_low, axis=0)
            sums = jnp.einsum("ijpq,jqs->ips", panel.astype(jnp.float32), earlier.astype(jnp.float32))
            rhs_level = rhs_level - sums
        solved = jnp.einsum("ipq,iqs->ips", inverse_all[start:start + LEVEL_BLOCKS], rhs_level,
                            precision=lax.Precision.HIGHEST)
        forward_vals.append(solved)
        forward_low.append(lax.optimization_barrier(solved.astype(jnp.bfloat16)))
    solution_parts = [None] * LEVELS
    later = []
    for level_id in reversed(range(LEVELS)):
        start = level_id * LEVEL_BLOCKS
        resid = forward_vals[level_id]
        if level_id < LEVELS - 1:
            panel = masked[(level_id + 1) * per_row:, :, level_id * COL_BLOCKS:(level_id + 1) * COL_BLOCKS, :]
            panel = panel.reshape((LEVELS - 1 - level_id) * LEVEL_BLOCKS, LEVEL_BLOCKS, BLOCK, BLOCK)
            after = jnp.concatenate(later, axis=0)
            sums = jnp.einsum("ijpq,ips->jqs", panel.astype(jnp.float32), after.astype(jnp.float32))
            resid = resid - sums
        solved = jnp.einsum("jqp,jqs->jps", inverse_all[start:start + LEVEL_BLOCKS], resid,
                            precision=lax.Precision.HIGHEST)
        solution_parts[level_id] = solved
        later = [lax.optimization_barrier(solved.astype(jnp.bfloat16))] + later
    solution = jnp.concatenate(solution_parts, axis=0)
    return solution.reshape(BLOCKS // N_COL, N_COL, BLOCK, SCENARIOS)
```

```python
import functools

import jax
import jax.numpy as jnp
from jax import lax
from jax.experimental import pallas as pl
from jax.experimental.pallas import tpu as pltpu
from jax.sharding import PartitionSpec as P

LEVELS = 8


def spread(value, axis, source):
    kept = jnp.where(lax.axis_index(axis) == source, value, 0).astype(value.dtype)
    return lax.psum(kept, axis)


def per_device(factor, pattern, loads, block_inverse):
    row_count = lax.axis_size("row")
    col_count = lax.axis_size("col")
    groups = col_count // row_count
    my_row = lax.axis_index("row")
    my_col = lax.axis_index("col")
    masked = factor[:, 0, :, 0] * pattern[:, 0, :, 0].astype(jnp.bfloat16)[:, :, None, None]
    per_row = factor.shape[0] // LEVELS
    per_col = factor.shape[2] // LEVELS
    rhs_local = loads[:, 0]
    inverse_local = block_inverse[:, 0]
    forward_vals = []
    forward_low = []
    for level_id in range(LEVELS):
        rhs_level = rhs_local[level_id * per_col : (level_id + 1) * per_col]
        inverse_level = inverse_local[level_id * per_col : (level_id + 1) * per_col]
        if level_id > 0:
            panel = masked[level_id * per_row : (level_id + 1) * per_row, : level_id * per_col]
            earlier = jnp.concatenate(forward_low, axis=0)
            partial_sum = jnp.einsum(
                "abpq,bqs->aps", panel, earlier, preferred_element_type=jnp.float32
            )
            row_total = lax.psum(partial_sum, "col")
            row_total = row_total.reshape((per_col, groups) + row_total.shape[1:])
            own_total = lax.dynamic_index_in_dim(
                row_total, my_col // row_count, axis=1, keepdims=False
            )
            solved = jnp.einsum(
                "mpq,mqs->mps",
                inverse_level,
                rhs_level - own_total,
                precision=lax.Precision.HIGHEST,
            )
            solved = spread(solved, "row", my_col % row_count)
        else:
            solved = jnp.einsum(
                "mpq,mqs->mps", inverse_level, rhs_level, precision=lax.Precision.HIGHEST
            )
        forward_vals.append(solved)
        forward_low.append(solved.astype(jnp.bfloat16))
    solution_parts = [None] * LEVELS
    later = []
    for level_id in reversed(range(LEVELS)):
        inverse_level = inverse_local[level_id * per_col : (level_id + 1) * per_col]
        resid = forward_vals[level_id]
        if level_id < LEVELS - 1:
            panel = masked[
                (level_id + 1) * per_row :, level_id * per_col : (level_id + 1) * per_col
            ]
            after = jnp.concatenate(later, axis=0)
            partial_sum = jnp.einsum(
                "abpq,aps->bqs", panel, after, preferred_element_type=jnp.float32
            )
            resid = resid - lax.psum(partial_sum, "row")
        solved = jnp.einsum("mqp,mqs->mps", inverse_level, resid, precision=lax.Precision.HIGHEST)
        solution_parts[level_id] = solved
        if level_id > 0:
            low_solved = solved.astype(jnp.bfloat16)
            pieces = lax.all_gather(low_solved[None], "col", axis=0, tiled=True)
            pieces = pieces.reshape((groups, row_count) + low_solved.shape)
            picked = lax.dynamic_index_in_dim(pieces, my_row, axis=1, keepdims=False)
            arranged = jnp.swapaxes(picked, 0, 1).reshape((per_row,) + low_solved.shape[1:])
            later = [arranged] + later
    solution = jnp.concatenate(solution_parts, axis=0)
    return solution[:, None]


MESH = pl.DeviceIdType.MESH
NT = (((1,), (1,)), ((), ()))
NN = (((1,), (0,)), ((), ()))
HIGHEST = lax.Precision.HIGHEST


def dot(a, b, dims, precision=None):
    return lax.dot_general(
        a, b, dims, precision=precision, preferred_element_type=jnp.float32
    )


def kernel(
    nz, nc, blk, scen, panel, loads, inverse, out,
    full, rhs, diag, yval, ylow, xlow, xout, part, sums, landed,
    own_sem, sib_sem_s, sib_sem_r, chip_sem_s, chip_sem_r,
    load_own, load_s, load_r, diag_own, diag_s, diag_r, diag_sib_s, diag_sib_r,
    y_s, y_r, p_s, p_r, out_s, out_r,
):
    groups = nc // nz
    chips = nc // 2
    span = groups * blk
    width = scen // nc
    z = lax.axis_index("row")
    c = lax.axis_index("col")
    chip = c // 2
    core = c % 2
    sibling = chip * 2 + 1 - core
    owner = c % nz == z
    relays = core == z % 2
    mine = c // nz

    def remote(src, dst, s, r, to):
        return pltpu.make_async_remote_copy(
            src_ref=src, dst_ref=dst, send_sem=s, recv_sem=r, device_id=to, device_id_type=MESH
        )

    barrier = pltpu.get_barrier_semaphore()
    for step in range(1, nz * nc):
        other = (z * nc + c + step) % (nz * nc)
        pl.semaphore_signal(
            barrier, inc=1, device_id=(other // nc, other % nc), device_id_type=MESH
        )
    pl.semaphore_wait(barrier, nz * nc - 1)

    def chunk(ref, level):
        return ref.at[pl.ds(level * span, span), pl.ds(0, level * blk)]

    def slot(col, level):
        return full.at[col, pl.ds(level * span, span), pl.ds(0, level * blk)]

    def load_copy(step):
        to = (c + step) % nc
        return remote(
            loads.at[:, pl.ds(to * width, width), :], rhs.at[mine],
            load_s.at[step], load_r.at[mine], (z, to),
        )

    def load_self():
        return pltpu.make_async_copy(
            loads.at[:, pl.ds(c * width, width), :], rhs.at[mine], load_own
        )

    def diag_copy(level, step):
        to = ((chip + step) % chips) * 2 + core
        return remote(
            inverse.at[level], diag.at[mine, level],
            diag_s.at[level, step], diag_r.at[level, mine], (z, to),
        )

    def diag_self(level):
        return pltpu.make_async_copy(
            inverse.at[level], diag.at[mine, level], diag_own.at[level]
        )

    def diag_sib(level, g):
        return remote(
            diag.at[g, level], diag.at[g, level],
            diag_sib_s.at[level, g], diag_sib_r.at[level, g], (z, sibling),
        )

    def chip_copy(level, step):
        to = ((chip + step) % chips) * 2 + core
        return remote(
            chunk(panel, level), slot(c, level),
            chip_sem_s.at[level, step], chip_sem_r.at[level, step], (z, to),
        )

    def own_copy(level):
        return pltpu.make_async_copy(chunk(panel, level), slot(c, level), own_sem.at[level])

    def sib_copy(level, step):
        if step == 0:
            src, col = chunk(panel, level), c
        else:
            col = ((chip + chips - step) % chips) * 2 + core
            src = slot(col, level)
        return remote(
            src, slot(col, level),
            sib_sem_s.at[level, step], sib_sem_r.at[level, step], (z, sibling),
        )

    @pl.when(owner)
    def _():
        load_self().start()
        for step in range(1, nc):
            load_copy(step).start()

    for level in range(LEVELS):
        @pl.when(owner)
        def _():
            diag_self(level).start()
            for step in range(1, chips):
                diag_copy(level, step).start()

        if level > 0:
            for step in range(1, chips):
                chip_copy(level, step).start()
            own_copy(level).start()
            sib_copy(level, 0).start()

    def relay(level):
        @pl.when(relays)
        def _():
            for g in range(groups):
                @pl.when(c == z + nz * g)
                def _():
                    diag_self(level).wait()

                @pl.when(c != z + nz * g)
                def _():
                    remote(
                        diag.at[g, level], diag.at[g, level], diag_s.at[level, 0],
                        diag_r.at[level, g], (z, sibling),
                    ).wait_recv()

                diag_sib(level, g).start()

        if level > 0:
            for step in range(1, chips):
                chip_copy(level, step).wait_recv()
                sib_copy(level, step).start()

    def arrived(level):
        @pl.when(jnp.logical_not(relays))
        def _():
            for g in range(groups):
                diag_sib(level, g).wait_recv()

        if level > 0:
            own_copy(level).wait()
            for step in range(chips):
                sib_copy(level, step).wait_recv()

    def y_copy(level, step):
        here = ylow.at[z, :, :, pl.ds(level * blk, blk)]
        return remote(
            here, here, y_s.at[level, step], y_r.at[level, step], ((z + step) % nz, c)
        )

    def column(col, low, high):
        return ylow[col % nz, col // nz, :, low * blk : high * blk]

    relay(0)
    for g in range(groups):
        @pl.when(c != z + nz * g)
        def _():
            remote(
                rhs.at[g], rhs.at[g], load_s.at[0], load_r.at[g], (z, sibling)
            ).wait_recv()

    @pl.when(owner)
    def _():
        load_self().wait()

    for level in range(LEVELS):
        arrived(level)
        if level > 0:
            total = jnp.zeros((width, span), jnp.float32)
            rows = pl.ds(level * span, span)
            if level > 1:
                def far(col, acc):
                    known = ylow[col % nz, col // nz, :, pl.ds(0, (level - 1) * blk)]
                    return acc + dot(known, full[col, rows, pl.ds(0, (level - 1) * blk)], NT)

                total = lax.fori_loop(0, nc, far, total)
            for step in range(1, nz):
                y_copy(level - 1, step).wait_recv()
            for col in range(nc):
                near = full[col, rows, pl.ds((level - 1) * blk, blk)]
                total = total + dot(column(col, level - 1, level), near, NT)
        for g in range(groups):
            resid = rhs[g, level]
            if level > 0:
                resid = resid - total[:, g * blk : (g + 1) * blk]
            solved = dot(resid, diag[g, level], NT, HIGHEST)
            yval[g, level] = solved
            if level < LEVELS - 1:
                ylow[z, g, :, level * blk : (level + 1) * blk] = solved.astype(jnp.bfloat16)
        if level < LEVELS - 1:
            for step in range(1, nz):
                y_copy(level, step).start()
            relay(level + 1)

    def part_copy(level, step):
        to = (z + step) % nz
        return remote(
            part.at[level, to], sums.at[level, z],
            p_s.at[level, step], p_r.at[level, step], (to, c),
        )

    def out_copy(level, step, g):
        return remote(
            xout.at[level, g], landed.at[level, c],
            out_s.at[level, step, g], out_r.at[level], ((z + step) % nz, z + nz * g),
        )

    def out_self(level, g):
        return pltpu.make_async_copy(xout.at[level, g], landed.at[level, c], out_r.at[level])

    for level in reversed(range(LEVELS)):
        if level < LEVELS - 1:
            lanes = pl.ds(level * blk, blk)
            first = (level + 1) * span
            second = first + span
            late = LEVELS * span
            near_x = xlow[:, first:second]
            for col in range(nc):
                value = dot(near_x, full[col, first:second, lanes], NN)
                if level < LEVELS - 2:
                    value = value + farsum[col]
                part[level, col % nz, col // nz] = value.astype(jnp.bfloat16)
            for step in range(1, nz):
                part_copy(level, step).start()
        if 0 < level:
            ahead = pl.ds((level - 1) * blk, blk)
        if level < LEVELS - 1:
            for step in range(1, nz):
                part_copy(level, step).wait_recv()
        for g in range(groups):
            resid = yval[g, level]
            if level < LEVELS - 1:
                for step in range(nz):
                    if step == 0:
                        piece = part[level, z, g]
                    else:
                        piece = sums[level, (z + nz - step) % nz, g]
                    resid = resid - piece.astype(jnp.float32)
            solved = dot(resid, diag[g, level], NN, HIGHEST)
            low = solved.astype(jnp.bfloat16)
            xout[level, g] = low
            if level > 0:
                at = level * span + g * blk
                xlow[:, at : at + blk] = low
        for g in range(groups):
            @pl.when(c == z + nz * g)
            def _():
                out_self(level, g).start()

            @pl.when(c != z + nz * g)
            def _():
                out_copy(level, 0, g).start()

            for step in range(1, nz):
                out_copy(level, step, g).start()
        if 0 < level < LEVELS - 1:
            low_row = (level + 1) * span
            known = xlow[:, low_row:]
            farsum = [dot(known, full[col, low_row:, ahead], NN) for col in range(nc)]

    for level in range(LEVELS):
        pltpu.make_async_copy(landed.at[level], landed.at[level], out_r.at[level]).wait()
    out[...] = landed[...]

    @pl.when(owner)
    def _():
        for step in range(1, nc):
            load_copy(step).wait_send()

    for level in range(LEVELS):
        @pl.when(owner)
        def _():
            for step in range(1, chips):
                diag_copy(level, step).wait_send()

        @pl.when(relays)
        def _():
            for g in range(groups):
                diag_sib(level, g).wait_send()

        if level > 0:
            for step in range(1, chips):
                chip_copy(level, step).wait_send()
            for step in range(chips):
                sib_copy(level, step).wait_send()
        if level < LEVELS - 1:
            for step in range(1, nz):
                y_copy(level, step).wait_send()
                part_copy(level, step).wait_send()
        for g in range(groups):
            @pl.when(c != z + nz * g)
            def _():
                out_copy(level, 0, g).wait_send()

            for step in range(1, nz):
                out_copy(level, step, g).wait_send()


def replicated_plan(factor, pattern, loads, block_inverse):
    nz, nc = lax.axis_size("row"), lax.axis_size("col")
    rows, cols, blk = factor.shape[0], factor.shape[2], factor.shape[4]
    scen = loads.shape[3]
    groups, chips, width = nc // nz, nc // 2, scen // nc
    masked = factor[:, 0, :, 0] * pattern[:, 0, :, 0].astype(jnp.bfloat16)[:, :, None, None]
    panel = jnp.swapaxes(masked, 1, 2).reshape(rows * blk, cols * blk)
    turned = jnp.swapaxes(loads[:, 0], 1, 2)
    low, f32 = jnp.bfloat16, jnp.float32
    dma = pltpu.SemaphoreType.DMA
    vmem = pl.BlockSpec(memory_space=pltpu.VMEM)
    result = pl.pallas_call(
        functools.partial(kernel, nz, nc, blk, scen),
        out_shape=jax.ShapeDtypeStruct((LEVELS, nc, width, blk), low),
        in_specs=[pl.BlockSpec(memory_space=pl.ANY), vmem, vmem],
        out_specs=vmem,
        scratch_shapes=[
            pltpu.VMEM((nc, rows * blk, cols * blk), low),
            pltpu.VMEM((groups, LEVELS, width, blk), f32),
            pltpu.VMEM((groups, LEVELS, blk, blk), f32),
            pltpu.VMEM((groups, LEVELS, width, blk), f32),
            pltpu.VMEM((nz, groups, width, LEVELS * blk), low),
            pltpu.VMEM((width, rows * blk), low),
            pltpu.VMEM((LEVELS, groups, width, blk), low),
            pltpu.VMEM((LEVELS, nz, groups, width, blk), low),
            pltpu.VMEM((LEVELS, nz, groups, width, blk), low),
            pltpu.VMEM((LEVELS, nc, width, blk), low),
            dma((LEVELS,)),
            dma((LEVELS, chips)), dma((LEVELS, chips)),
            dma((LEVELS, chips)), dma((LEVELS, chips)),
            dma, dma((nc,)), dma((groups,)),
            dma((LEVELS,)), dma((LEVELS, chips)), dma((LEVELS, groups)),
            dma((LEVELS, groups)), dma((LEVELS, groups)),
            dma((LEVELS, nz)), dma((LEVELS, nz)),
            dma((LEVELS, nz)), dma((LEVELS, nz)),
            dma((LEVELS, nz, groups)), dma((LEVELS,)),
        ],
        compiler_params=pltpu.CompilerParams(
            collective_id=0, has_side_effects=True, vmem_limit_bytes=52 * 2**20
        ),
    )(panel, turned, block_inverse[:, 0])
    result = result.reshape(LEVELS, scen, blk).astype(f32)
    return jnp.swapaxes(result, 1, 2)[:, None]


def pick_plan(mesh):
    def plan(factor, pattern, loads, block_inverse):
        nz, nc = mesh.shape["row"], mesh.shape["col"]
        scen = loads.shape[3]
        small = nc * factor.size * 2 <= 32 * 2**20
        even = nc % nz == 0 and nc % 2 == 0 and nz % 2 == 0 and scen % (16 * nc) == 0
        if small and even and loads.shape[0] == LEVELS:
            return replicated_plan(factor, pattern, loads, block_inverse)
        return per_device(factor, pattern, loads, block_inverse)

    return plan


def solution(mesh):
    in_specs = (
        P(None, "row", None, "col", None, None),
        P(None, "row", None, "col"),
        P(None, "col", None, None),
        P(None, "col", None, None),
    )
    out_specs = P(None, "col", None, None)
    return jax.shard_map(
        pick_plan(mesh), mesh=mesh, in_specs=in_specs, out_specs=out_specs, check_vma=False
    )
```

```python
import functools

import jax
import jax.numpy as jnp
from jax import lax
from jax.experimental import pallas as pl
from jax.experimental.pallas import tpu as pltpu
from jax.sharding import PartitionSpec as P

LEVELS = 8


def spread(value, axis, source):
    kept = jnp.where(lax.axis_index(axis) == source, value, 0).astype(value.dtype)
    return lax.psum(kept, axis)


def per_device(factor, pattern, loads, block_inverse):
    row_count = lax.axis_size("row")
    col_count = lax.axis_size("col")
    groups = col_count // row_count
    my_row = lax.axis_index("row")
    my_col = lax.axis_index("col")
    masked = factor[:, 0, :, 0] * pattern[:, 0, :, 0].astype(jnp.bfloat16)[:, :, None, None]
    per_row = factor.shape[0] // LEVELS
    per_col = factor.shape[2] // LEVELS
    rhs_local = loads[:, 0]
    inverse_local = block_inverse[:, 0]
    forward_vals = []
    forward_low = []
    for level_id in range(LEVELS):
        rhs_level = rhs_local[level_id * per_col : (level_id + 1) * per_col]
        inverse_level = inverse_local[level_id * per_col : (level_id + 1) * per_col]
        if level_id > 0:
            panel = masked[level_id * per_row : (level_id + 1) * per_row, : level_id * per_col]
            earlier = jnp.concatenate(forward_low, axis=0)
            partial_sum = jnp.einsum(
                "abpq,bqs->aps", panel, earlier, preferred_element_type=jnp.float32
            )
            row_total = lax.psum(partial_sum, "col")
            row_total = row_total.reshape((per_col, groups) + row_total.shape[1:])
            own_total = lax.dynamic_index_in_dim(
                row_total, my_col // row_count, axis=1, keepdims=False
            )
            solved = jnp.einsum(
                "mpq,mqs->mps",
                inverse_level,
                rhs_level - own_total,
                precision=lax.Precision.HIGHEST,
            )
            solved = spread(solved, "row", my_col % row_count)
        else:
            solved = jnp.einsum(
                "mpq,mqs->mps", inverse_level, rhs_level, precision=lax.Precision.HIGHEST
            )
        forward_vals.append(solved)
        forward_low.append(solved.astype(jnp.bfloat16))
    solution_parts = [None] * LEVELS
    later = []
    for level_id in reversed(range(LEVELS)):
        inverse_level = inverse_local[level_id * per_col : (level_id + 1) * per_col]
        resid = forward_vals[level_id]
        if level_id < LEVELS - 1:
            panel = masked[
                (level_id + 1) * per_row :, level_id * per_col : (level_id + 1) * per_col
            ]
            after = jnp.concatenate(later, axis=0)
            partial_sum = jnp.einsum(
                "abpq,aps->bqs", panel, after, preferred_element_type=jnp.float32
            )
            resid = resid - lax.psum(partial_sum, "row")
        solved = jnp.einsum("mqp,mqs->mps", inverse_level, resid, precision=lax.Precision.HIGHEST)
        solution_parts[level_id] = solved
        if level_id > 0:
            low_solved = solved.astype(jnp.bfloat16)
            pieces = lax.all_gather(low_solved[None], "col", axis=0, tiled=True)
            pieces = pieces.reshape((groups, row_count) + low_solved.shape)
            picked = lax.dynamic_index_in_dim(pieces, my_row, axis=1, keepdims=False)
            arranged = jnp.swapaxes(picked, 0, 1).reshape((per_row,) + low_solved.shape[1:])
            later = [arranged] + later
    solution = jnp.concatenate(solution_parts, axis=0)
    return solution[:, None]


MESH = pl.DeviceIdType.MESH
NT = (((1,), (1,)), ((), ()))
NN = (((1,), (0,)), ((), ()))
HIGHEST = lax.Precision.HIGHEST


def dot(a, b, dims, precision=None):
    return lax.dot_general(
        a, b, dims, precision=precision, preferred_element_type=jnp.float32
    )


def kernel(
    nz, nc, blk, scen, factor, pattern, loads, inverse, out,
    near, own, rhs, diag, yval, ylow, yfull, fpart, fsum, xlow, xfull,
    part, sums, bpart, bsum, landed,
    sib_s, sib_r, chip_s, chip_r,
    load_own, load_s, load_r, diag_own, diag_s, diag_r, diag_sib_s, diag_sib_r,
    y_s, y_r, yf_s, yf_r, f_s, f_r, p_s, p_r, xf_s, xf_r, b_s, b_r, out_s, out_r,
):
    groups = nc // nz
    chips = nc // 2
    width = scen // nc
    last = LEVELS - 1
    z = lax.axis_index("row")
    c = lax.axis_index("col")
    chip = c // 2
    core = c % 2
    sibling = chip * 2 + 1 - core
    owner = c % nz == z
    relays = core == z % 2
    mine = c // nz

    def remote(src, dst, s, r, to):
        return pltpu.make_async_remote_copy(
            src_ref=src, dst_ref=dst, send_sem=s, recv_sem=r, device_id=to, device_id_type=MESH
        )

    def share(col):
        return pl.ds(pl.multiple_of(col * width, width), width)

    def masked(row, col):
        return factor[row, col] * pattern[row, col].astype(jnp.float32).astype(jnp.bfloat16)

    for level in range(1, LEVELS):
        for g in range(groups):
            near[c, level, g * blk : (g + 1) * blk] = masked(level * groups + g, level - 1)

    barrier = pltpu.get_barrier_semaphore()
    for step in range(1, nz * nc):
        other = (z * nc + c + step) % (nz * nc)
        pl.semaphore_signal(
            barrier, inc=1, device_id=(other // nc, other % nc), device_id_type=MESH
        )
    pl.semaphore_wait(barrier, nz * nc - 1)

    def load_copy(step):
        to = (c + step) % nc
        return remote(
            loads.at[:, share(to), :], rhs.at[mine],
            load_s.at[step], load_r.at[mine], (z, to),
        )

    def load_self():
        return pltpu.make_async_copy(loads.at[:, share(c), :], rhs.at[mine], load_own)

    def diag_copy(level, step):
        to = ((chip + step) % chips) * 2 + core
        return remote(
            inverse.at[level], diag.at[mine, level],
            diag_s.at[level, step], diag_r.at[level, mine], (z, to),
        )

    def diag_self(level):
        return pltpu.make_async_copy(
            inverse.at[level], diag.at[mine, level], diag_own.at[level]
        )

    def diag_sib(level, g):
        return remote(
            diag.at[g, level], diag.at[g, level],
            diag_sib_s.at[level, g], diag_sib_r.at[level, g], (z, sibling),
        )

    def chip_copy(level, step):
        to = ((chip + step) % chips) * 2 + core
        here = near.at[c, level]
        return remote(here, here, chip_s.at[level, step], chip_r.at[level, step], (z, to))

    def sib_copy(level, step):
        here = near.at[((chip + chips - step) % chips) * 2 + core, level]
        return remote(here, here, sib_s.at[level, step], sib_r.at[level, step], (z, sibling))

    @pl.when(owner)
    def _():
        load_self().start()
        for step in range(1, nc):
            load_copy(step).start()

    for level in range(LEVELS):
        @pl.when(owner)
        def _():
            diag_self(level).start()
            for step in range(1, chips):
                diag_copy(level, step).start()

        if level > 0:
            for step in range(1, chips):
                chip_copy(level, step).start()
            sib_copy(level, 0).start()

    for level in range(2, LEVELS):
        for g in range(groups):
            for col in range(level - 1):
                own[level * groups + g, col] = masked(level * groups + g, col)

    def relay(level):
        @pl.when(relays)
        def _():
            for g in range(groups):
                @pl.when(c == z + nz * g)
                def _():
                    diag_self(level).wait()

                @pl.when(c != z + nz * g)
                def _():
                    remote(
                        diag.at[g, level], diag.at[g, level], diag_s.at[level, 0],
                        diag_r.at[level, g], (z, sibling),
                    ).wait_recv()

                diag_sib(level, g).start()

        if level > 0:
            for step in range(1, chips):
                chip_copy(level, step).wait_recv()
                sib_copy(level, step).start()

    def arrived(level):
        @pl.when(jnp.logical_not(relays))
        def _():
            for g in range(groups):
                diag_sib(level, g).wait_recv()

        if level > 0:
            for step in range(chips):
                sib_copy(level, step).wait_recv()

    def spread_sent(level):
        @pl.when(owner)
        def _():
            for step in range(1, chips):
                diag_copy(level, step).wait_send()

        @pl.when(relays)
        def _():
            for g in range(groups):
                diag_sib(level, g).wait_send()

        if level > 0:
            for step in range(1, chips):
                chip_copy(level, step).wait_send()
            for step in range(chips):
                sib_copy(level, step).wait_send()

    def y_copy(level, step):
        here = ylow.at[level, z]
        return remote(
            here, here, y_s.at[level, step], y_r.at[level, step], ((z + step) % nz, c)
        )

    def to_columns(src, dst, s, r, act):
        for g in range(groups):
            for step in range(nz):
                def go():
                    copy = remote(
                        src.at[g], dst, s.at[step, g], r, ((z + step) % nz, z + nz * g)
                    )
                    copy.start() if act else copy.wait_send()

                if step > 0:
                    go()
                else:
                    pl.when(c != z + nz * g)(go)
                    if act:
                        @pl.when(c == z + nz * g)
                        def _():
                            pltpu.make_async_copy(src.at[g], dst, r).start()

    def y_far(level, act):
        to_columns(
            ylow.at[level, z], yfull.at[level, share(c), :], yf_s.at[level], yf_r.at[level], act
        )

    def out_far(level, act):
        to_columns(xlow.at[level], landed.at[level, c], out_s.at[level], out_r.at[level], act)

    def f_far(level, act):
        for step in range(1, nc):
            to = (c + step) % nc
            copy = remote(
                fpart.at[level, :, share(to), :], fsum.at[level, c],
                f_s.at[level, step], f_r.at[level], (z, to),
            )
            copy.start() if act else copy.wait_send()
        if act:
            pltpu.make_async_copy(
                fpart.at[level, :, share(c), :], fsum.at[level, c], f_r.at[level]
            ).start()

    def x_far(level, act):
        here = xfull.at[level, :, share(c), :]
        for step in range(1, nc):
            copy = remote(
                xlow.at[level], here, xf_s.at[level, step], xf_r.at[level], (z, (c + step) % nc)
            )
            copy.start() if act else copy.wait_send()
        if act:
            pltpu.make_async_copy(xlow.at[level], here, xf_r.at[level]).start()

    def b_far(level, act):
        for step in range(nc):
            to = (c + step) % nc
            src, dst = bpart.at[level, share(to), :], bsum.at[level, z, mine]

            def go():
                copy = remote(src, dst, b_s.at[level, step], b_r.at[level], (c % nz, to))
                copy.start() if act else copy.wait_send()

            if step > 0:
                go()
            else:
                pl.when(jnp.logical_not(owner))(go)
                if act:
                    @pl.when(owner)
                    def _():
                        pltpu.make_async_copy(src, dst, b_r.at[level]).start()

    def all_in(ref, sem):
        pltpu.make_async_copy(ref, ref, sem).wait()

    relay(0)
    for g in range(groups):
        @pl.when(c != z + nz * g)
        def _():
            remote(
                rhs.at[g], rhs.at[g], load_s.at[0], load_r.at[g], (z, sibling)
            ).wait_recv()

    @pl.when(owner)
    def _():
        load_self().wait()

    for level in range(LEVELS):
        arrived(level)
        resid = [rhs[g, level] for g in range(groups)]
        if level > 1:
            all_in(fsum.at[level], f_r.at[level])
            for g in range(groups):
                for col in range(nc):
                    resid[g] = resid[g] - fsum[level, col, g].astype(jnp.float32)
        if level > 0:
            for step in range(1, nz):
                y_copy(level - 1, step).wait_recv()
            total = jnp.zeros((width, groups * blk), jnp.float32)
            for col in range(nc):
                total = total + dot(ylow[level - 1, col % nz, col // nz], near[col, level], NT)
            resid = [resid[g] - total[:, g * blk : (g + 1) * blk] for g in range(groups)]
        for g in range(groups):
            solved = dot(resid[g], diag[g, level], NT, HIGHEST)
            yval[g, level] = solved
            if level < last:
                ylow[level, z, g] = solved.astype(jnp.bfloat16)
        if level < last:
            for step in range(1, nz):
                y_copy(level, step).start()
            if level > 0:
                all_in(yfull.at[level - 1], yf_r.at[level - 1])
                for g in range(groups):
                    row = (level + 1) * groups + g
                    value = dot(yfull[0], own[row, 0], NT)
                    for col in range(1, level):
                        value = value + dot(yfull[col], own[row, col], NT)
                    fpart[level + 1, g] = value.astype(jnp.bfloat16)
                f_far(level + 1, True)
            if level < last - 1:
                y_far(level, True)
            relay(level + 1)
            if level > 0:
                for step in range(1, nz):
                    y_copy(level - 1, step).wait_send()
                y_far(level - 1, False)
                spread_sent(level - 1)
            if level > 1:
                f_far(level, False)

    def part_copy(level, step):
        to = (z + step) % nz
        return remote(
            part.at[level, to], sums.at[level, z],
            p_s.at[level, step], p_r.at[level, step], (to, c),
        )

    for level in reversed(range(LEVELS)):
        if level < last:
            above = jnp.concatenate([xlow[level + 1, g] for g in range(groups)], axis=1)
            for col in range(nc):
                value = dot(above, near[col, level + 1], NN)
                part[level, col % nz, col // nz] = value.astype(jnp.bfloat16)
            for step in range(1, nz):
                part_copy(level, step).start()
            if level < last - 1:
                all_in(xfull.at[level + 2], xf_r.at[level + 2])
                value = None
                for up in range(level + 2, LEVELS):
                    for g in range(groups):
                        term = dot(xfull[up, g], own[up * groups + g, level], NN)
                        value = term if value is None else value + term
                bpart[level] = value.astype(jnp.bfloat16)
                b_far(level, True)
            if level > 0:
                x_far(level + 1, True)
            out_far(level + 1, True)
            if level == last - 1:
                for step in range(1, nz):
                    y_copy(last - 1, step).wait_send()
                f_far(last, False)
                spread_sent(last - 1)
                spread_sent(last)

                @pl.when(owner)
                def _():
                    for step in range(1, nc):
                        load_copy(step).wait_send()
            else:
                for step in range(1, nz):
                    part_copy(level + 1, step).wait_send()
                x_far(level + 2, False)
                out_far(level + 2, False)
                all_in(landed.at[level + 2], out_r.at[level + 2])
            if level < last - 2:
                b_far(level + 1, False)
            for step in range(1, nz):
                part_copy(level, step).wait_recv()
            if level < last - 1:
                all_in(bsum.at[level], b_r.at[level])
        for g in range(groups):
            resid = yval[g, level]
            if level < last:
                for step in range(nz):
                    if step == 0:
                        piece = part[level, z, g]
                    else:
                        piece = sums[level, (z + nz - step) % nz, g]
                    resid = resid - piece.astype(jnp.float32)
                    if level < last - 1:
                        resid = resid - bsum[level, step, g].astype(jnp.float32)
            xlow[level, g] = dot(resid, diag[g, level], NN, HIGHEST).astype(jnp.bfloat16)

    out_far(0, True)
    for step in range(1, nz):
        part_copy(0, step).wait_send()
    b_far(0, False)
    out_far(1, False)
    all_in(landed.at[1], out_r.at[1])
    out[1:] = landed[1:]
    out_far(0, False)
    all_in(landed.at[0], out_r.at[0])
    out[0] = landed[0]


def split_plan(factor, pattern, loads, block_inverse):
    nz, nc = lax.axis_size("row"), lax.axis_size("col")
    rows, cols, blk = factor.shape[0], factor.shape[2], factor.shape[4]
    scen = loads.shape[3]
    groups, chips, width = nc // nz, nc // 2, scen // nc
    turned = jnp.swapaxes(loads[:, 0], 1, 2)
    low, f32 = jnp.bfloat16, jnp.float32
    dma = pltpu.SemaphoreType.DMA
    vmem = pl.BlockSpec(memory_space=pltpu.VMEM)
    smem = pl.BlockSpec(memory_space=pltpu.SMEM)
    result = pl.pallas_call(
        functools.partial(kernel, nz, nc, blk, scen),
        out_shape=jax.ShapeDtypeStruct((LEVELS, nc, width, blk), low),
        in_specs=[vmem, smem, vmem, vmem],
        out_specs=vmem,
        scratch_shapes=[
            pltpu.VMEM((nc, LEVELS, groups * blk, blk), low),
            pltpu.VMEM((rows, cols, blk, blk), low),
            pltpu.VMEM((groups, LEVELS, width, blk), f32),
            pltpu.VMEM((groups, LEVELS, blk, blk), f32),
            pltpu.VMEM((groups, LEVELS, width, blk), f32),
            pltpu.VMEM((LEVELS, nz, groups, width, blk), low),
            pltpu.VMEM((LEVELS, scen, blk), low),
            pltpu.VMEM((LEVELS, groups, scen, blk), low),
            pltpu.VMEM((LEVELS, nc, groups, width, blk), low),
            pltpu.VMEM((LEVELS, groups, width, blk), low),
            pltpu.VMEM((LEVELS, groups, scen, blk), low),
            pltpu.VMEM((LEVELS, nz, groups, width, blk), low),
            pltpu.VMEM((LEVELS, nz, groups, width, blk), low),
            pltpu.VMEM((LEVELS, scen, blk), low),
            pltpu.VMEM((LEVELS, nz, groups, width, blk), low),
            pltpu.VMEM((LEVELS, nc, width, blk), low),
            dma((LEVELS, chips)), dma((LEVELS, chips)),
            dma((LEVELS, chips)), dma((LEVELS, chips)),
            dma, dma((nc,)), dma((groups,)),
            dma((LEVELS,)), dma((LEVELS, chips)), dma((LEVELS, groups)),
            dma((LEVELS, groups)), dma((LEVELS, groups)),
            dma((LEVELS, nz)), dma((LEVELS, nz)),
            dma((LEVELS, nz, groups)), dma((LEVELS,)),
            dma((LEVELS, nc)), dma((LEVELS,)),
            dma((LEVELS, nz)), dma((LEVELS, nz)),
            dma((LEVELS, nc)), dma((LEVELS,)),
            dma((LEVELS, nc)), dma((LEVELS,)),
            dma((LEVELS, nz, groups)), dma((LEVELS,)),
        ],
        compiler_params=pltpu.CompilerParams(
            collective_id=0, has_side_effects=True, vmem_limit_bytes=52 * 2**20
        ),
    )(factor[:, 0, :, 0], pattern[:, 0, :, 0], turned, block_inverse[:, 0])
    result = result.reshape(LEVELS, scen, blk).astype(f32)
    return jnp.swapaxes(result, 1, 2)[:, None]


def pick_plan(mesh):
    def plan(factor, pattern, loads, block_inverse):
        nz, nc = mesh.shape["row"], mesh.shape["col"]
        scen = loads.shape[3]
        small = nc * factor.size * 2 <= 32 * 2**20
        single = factor.shape[2] == LEVELS and factor.shape[0] == LEVELS * (nc // nz)
        even = nc % nz == 0 and nc % 2 == 0 and nz % 2 == 0 and scen % (16 * nc) == 0
        if small and even and single and loads.shape[0] == LEVELS:
            return split_plan(factor, pattern, loads, block_inverse)
        return per_device(factor, pattern, loads, block_inverse)

    return plan


def solution(mesh):
    in_specs = (
        P(None, "row", None, "col", None, None),
        P(None, "row", None, "col"),
        P(None, "col", None, None),
        P(None, "col", None, None),
    )
    out_specs = P(None, "col", None, None)
    return jax.shard_map(
        pick_plan(mesh), mesh=mesh, in_specs=in_specs, out_specs=out_specs, check_vma=False
    )
```

```python
import functools

import jax
import jax.numpy as jnp
from jax import lax
from jax.experimental import pallas as pl
from jax.experimental.pallas import tpu as pltpu
from jax.sharding import PartitionSpec as P

LEVELS = 8


def spread(value, axis, source):
    kept = jnp.where(lax.axis_index(axis) == source, value, 0).astype(value.dtype)
    return lax.psum(kept, axis)


def per_device(factor, pattern, loads, block_inverse):
    row_count = lax.axis_size("row")
    col_count = lax.axis_size("col")
    groups = col_count // row_count
    my_row = lax.axis_index("row")
    my_col = lax.axis_index("col")
    masked = factor[:, 0, :, 0] * pattern[:, 0, :, 0].astype(jnp.bfloat16)[:, :, None, None]
    per_row = factor.shape[0] // LEVELS
    per_col = factor.shape[2] // LEVELS
    rhs_local = loads[:, 0]
    inverse_local = block_inverse[:, 0]
    forward_vals = []
    forward_low = []
    for level_id in range(LEVELS):
        rhs_level = rhs_local[level_id * per_col : (level_id + 1) * per_col]
        inverse_level = inverse_local[level_id * per_col : (level_id + 1) * per_col]
        if level_id > 0:
            panel = masked[level_id * per_row : (level_id + 1) * per_row, : level_id * per_col]
            earlier = jnp.concatenate(forward_low, axis=0)
            partial_sum = jnp.einsum(
                "abpq,bqs->aps", panel, earlier, preferred_element_type=jnp.float32
            )
            row_total = lax.psum(partial_sum, "col")
            row_total = row_total.reshape((per_col, groups) + row_total.shape[1:])
            own_total = lax.dynamic_index_in_dim(
                row_total, my_col // row_count, axis=1, keepdims=False
            )
            solved = jnp.einsum(
                "mpq,mqs->mps",
                inverse_level,
                rhs_level - own_total,
                precision=lax.Precision.HIGHEST,
            )
            solved = spread(solved, "row", my_col % row_count)
        else:
            solved = jnp.einsum(
                "mpq,mqs->mps", inverse_level, rhs_level, precision=lax.Precision.HIGHEST
            )
        forward_vals.append(solved)
        forward_low.append(solved.astype(jnp.bfloat16))
    solution_parts = [None] * LEVELS
    later = []
    for level_id in reversed(range(LEVELS)):
        inverse_level = inverse_local[level_id * per_col : (level_id + 1) * per_col]
        resid = forward_vals[level_id]
        if level_id < LEVELS - 1:
            panel = masked[
                (level_id + 1) * per_row :, level_id * per_col : (level_id + 1) * per_col
            ]
            after = jnp.concatenate(later, axis=0)
            partial_sum = jnp.einsum(
                "abpq,aps->bqs", panel, after, preferred_element_type=jnp.float32
            )
            resid = resid - lax.psum(partial_sum, "row")
        solved = jnp.einsum("mqp,mqs->mps", inverse_level, resid, precision=lax.Precision.HIGHEST)
        solution_parts[level_id] = solved
        if level_id > 0:
            low_solved = solved.astype(jnp.bfloat16)
            pieces = lax.all_gather(low_solved[None], "col", axis=0, tiled=True)
            pieces = pieces.reshape((groups, row_count) + low_solved.shape)
            picked = lax.dynamic_index_in_dim(pieces, my_row, axis=1, keepdims=False)
            arranged = jnp.swapaxes(picked, 0, 1).reshape((per_row,) + low_solved.shape[1:])
            later = [arranged] + later
    solution = jnp.concatenate(solution_parts, axis=0)
    return solution[:, None]


MESH = pl.DeviceIdType.MESH
NT = (((1,), (1,)), ((), ()))
NN = (((1,), (0,)), ((), ()))


def dot(a, b, dims):
    return lax.dot_general(a, b, dims, preferred_element_type=jnp.float32)


def kernel(
    nz, nc, blk, scen, factor, pattern, loads, inverse, out,
    turned, split, near, own, rhs, diag, yval, ylow, yfull, fpart, fsum, xlow, xfull,
    part, sums, bpart, bsum, landed,
    sib_s, sib_r, chip_s, chip_r,
    load_own, load_s, load_r, diag_own, diag_s, diag_r, diag_sib_s, diag_sib_r,
    y_s, y_r, yf_s, yf_r, f_s, f_r, p_s, p_r, xf_s, xf_r, b_s, b_r, out_s, out_r,
):
    groups = nc // nz
    chips = nc // 2
    width = scen // nc
    last = LEVELS - 1
    z = lax.axis_index("row")
    c = lax.axis_index("col")
    chip = c // 2
    core = c % 2
    sibling = chip * 2 + 1 - core
    owner = c % nz == z
    relays = core == z % 2
    mine = c // nz
    span = groups * blk
    place = (c % nz) * groups + c // nz
    cuts = ((0, 1), (1, 3), (3, LEVELS))

    barrier = pltpu.get_barrier_semaphore()
    for step in range(1, nz * nc):
        other = (z * nc + c + step) % (nz * nc)
        pl.semaphore_signal(
            barrier, inc=1, device_id=(other // nc, other % nc), device_id_type=MESH
        )

    def remote(src, dst, s, r, to):
        return pltpu.make_async_remote_copy(
            src_ref=src, dst_ref=dst, send_sem=s, recv_sem=r, device_id=to, device_id_type=MESH
        )

    def share(col):
        return pl.ds(pl.multiple_of(col * width, width), width)

    def masked(row, col):
        return factor[row, col] * pattern[row, col].astype(jnp.float32).astype(jnp.bfloat16)

    def lane(index, size):
        return pl.ds(pl.multiple_of(index * size, size), size)

    def turn(level):
        turned[level] = loads[level].T

    def halves(value):
        high = value.astype(jnp.bfloat16)
        return high, (value - high.astype(jnp.float32)).astype(jnp.bfloat16)

    for level in range(LEVELS):
        high, rest = halves(inverse[level])
        split[level, :, :blk] = high
        split[level, :, blk:] = rest
    for level in range(1, LEVELS):
        for g in range(groups):
            rows = slice(g * blk, (g + 1) * blk)
            near[level, rows, lane(place, blk)] = masked(level * groups + g, level - 1)
    turn(0)
    pl.semaphore_wait(barrier, nz * nc - 1)

    def load_copy(cut, step):
        to = (c + step) % nc
        levels = pl.ds(cuts[cut][0], cuts[cut][1] - cuts[cut][0])
        return remote(
            turned.at[levels, share(to), :], rhs.at[mine, levels],
            load_s.at[cut, step], load_r.at[cut, mine], (z, to),
        )

    def load_self(cut):
        levels = pl.ds(cuts[cut][0], cuts[cut][1] - cuts[cut][0])
        return pltpu.make_async_copy(
            turned.at[levels, share(c), :], rhs.at[mine, levels], load_own.at[cut]
        )

    def load_start(cut):
        @pl.when(owner)
        def _():
            load_self(cut).start()
            for step in range(1, nc):
                load_copy(cut, step).start()

    def load_wait(cut):
        levels = pl.ds(cuts[cut][0], cuts[cut][1] - cuts[cut][0])
        for g in range(groups):
            @pl.when(c != z + nz * g)
            def _():
                here = rhs.at[g, levels]
                remote(
                    here, here, load_s.at[cut, 0], load_r.at[cut, g], (z, sibling)
                ).wait_recv()

        @pl.when(owner)
        def _():
            load_self(cut).wait()

    def diag_copy(level, step):
        to = ((chip + step) % chips) * 2 + core
        return remote(
            split.at[level], diag.at[mine, level],
            diag_s.at[level, step], diag_r.at[level, mine], (z, to),
        )

    def diag_self(level):
        return pltpu.make_async_copy(
            split.at[level], diag.at[mine, level], diag_own.at[level]
        )

    def diag_sib(level, g):
        return remote(
            diag.at[g, level], diag.at[g, level],
            diag_sib_s.at[level, g], diag_sib_r.at[level, g], (z, sibling),
        )

    def chip_copy(level, step):
        to = ((chip + step) % chips) * 2 + core
        here = near.at[level, :, lane(place, blk)]
        return remote(here, here, chip_s.at[level, step], chip_r.at[level, step], (z, to))

    def sib_copy(level, step):
        col = ((chip + chips - step) % chips) * 2 + core
        here = near.at[level, :, lane((col % nz) * groups + col // nz, blk)]
        return remote(here, here, sib_s.at[level, step], sib_r.at[level, step], (z, sibling))

    def spread(level):
        @pl.when(owner)
        def _():
            diag_self(level).start()
            for step in range(1, chips):
                diag_copy(level, step).start()

        if level > 0:
            for step in range(1, chips):
                chip_copy(level, step).start()
            sib_copy(level, 0).start()

    load_start(0)
    spread(0)
    spread(1)
    for level in range(1, LEVELS):
        turn(level)
    load_start(1)
    spread(2)
    for level in range(2, LEVELS):
        for g in range(groups):
            for col in range(level - 1):
                block = masked(level * groups + g, col)
                own[level, g * blk : (g + 1) * blk, col * blk : (col + 1) * blk] = block

    def relay(level):
        @pl.when(relays)
        def _():
            for g in range(groups):
                @pl.when(c == z + nz * g)
                def _():
                    diag_self(level).wait()

                @pl.when(c != z + nz * g)
                def _():
                    remote(
                        diag.at[g, level], diag.at[g, level], diag_s.at[level, 0],
                        diag_r.at[level, g], (z, sibling),
                    ).wait_recv()

                diag_sib(level, g).start()

        if level > 0:
            for step in range(1, chips):
                chip_copy(level, step).wait_recv()
                sib_copy(level, step).start()

    def arrived(level):
        @pl.when(jnp.logical_not(relays))
        def _():
            for g in range(groups):
                diag_sib(level, g).wait_recv()

        if level > 0:
            for step in range(chips):
                sib_copy(level, step).wait_recv()

    def spread_sent(level):
        @pl.when(owner)
        def _():
            for step in range(1, chips):
                diag_copy(level, step).wait_send()

        @pl.when(relays)
        def _():
            for g in range(groups):
                diag_sib(level, g).wait_send()

        if level > 0:
            for step in range(1, chips):
                chip_copy(level, step).wait_send()
            for step in range(chips):
                sib_copy(level, step).wait_send()

    def y_copy(level, step):
        here = ylow.at[level, :, lane(z, span)]
        return remote(
            here, here, y_s.at[level, step], y_r.at[level, step], ((z + step) % nz, c)
        )

    def to_columns(source, dst, s, r, act):
        for g in range(groups):
            src = source(g)

            for step in range(nz):
                def go():
                    copy = remote(
                        src, dst, s.at[step, g], r, ((z + step) % nz, z + nz * g)
                    )
                    copy.start() if act else copy.wait_send()

                if step > 0:
                    go()
                else:
                    pl.when(c != z + nz * g)(go)
                    if act:
                        @pl.when(c == z + nz * g)
                        def _():
                            pltpu.make_async_copy(src, dst, r).start()

    def y_far(level, act):
        to_columns(
            lambda g: ylow.at[level, :, lane(z * groups + g, blk)],
            yfull.at[share(c), pl.ds(level * blk, blk)],
            yf_s.at[level], yf_r.at[level], act,
        )

    def out_far(level, act):
        pair = pl.ds(level, 2)
        to_columns(
            lambda g: xlow.at[pair, :, pl.ds(g * blk, blk)], landed.at[pair, c],
            out_s.at[level], out_r.at[level], act,
        )

    def f_far(level, act):
        for step in range(1, nc):
            to = (c + step) % nc
            copy = remote(
                fpart.at[level, share(to), :], fsum.at[level, step - 1],
                f_s.at[level, step], f_r.at[level], (z, to),
            )
            copy.start() if act else copy.wait_send()

    def x_far(level, act):
        here = xfull.at[level, share(c), :]
        for step in range(1, nc):
            copy = remote(
                xlow.at[level], here, xf_s.at[level, step], xf_r.at[level], (z, (c + step) % nc)
            )
            copy.start() if act else copy.wait_send()
        if act:
            pltpu.make_async_copy(xlow.at[level], here, xf_r.at[level]).start()

    def b_far(level, act):
        for step in range(nc):
            to = (c + step) % nc
            src, dst = bpart.at[level, share(to), :], bsum.at[level, z, :, lane(mine, blk)]

            def go():
                copy = remote(src, dst, b_s.at[level, step], b_r.at[level], (c % nz, to))
                copy.start() if act else copy.wait_send()

            if step > 0:
                go()
            else:
                pl.when(jnp.logical_not(owner))(go)
                if act:
                    @pl.when(owner)
                    def _():
                        pltpu.make_async_copy(src, dst, b_r.at[level]).start()

    def all_in(ref, sem):
        pltpu.make_async_copy(ref, ref, sem).wait()

    def apply(value, low, rest, dims):
        axis = dims[0][1][0]
        high, small = halves(value)
        left = jnp.concatenate([high, small, high], axis=1)
        return dot(left, jnp.concatenate([low, low, rest], axis=axis), dims)

    def solve(level, value, dims):
        return [
            apply(
                value[:, g * blk : (g + 1) * blk],
                diag[g, level, :, :blk], diag[g, level, :, blk:], dims,
            )
            for g in range(groups)
        ]

    relay(0)
    load_wait(0)

    for level in range(LEVELS):
        for cut in range(1, len(cuts)):
            if level == cuts[cut][0]:
                load_wait(cut)
        arrived(level)
        resid = jnp.concatenate([rhs[g, level] for g in range(groups)], axis=1)
        if level > 1:
            all_in(fsum.at[level], f_r.at[level])
            resid = resid - fpart[level, share(c), :].astype(jnp.float32)
            for step in range(nc - 1):
                resid = resid - fsum[level, step].astype(jnp.float32)
        if level > 0:
            for step in range(1, nz):
                y_copy(level - 1, step).wait_recv()
            resid = resid - dot(ylow[level - 1], near[level], NT)
        solved = jnp.concatenate(solve(level, resid, NT), axis=1)
        yval[level] = solved
        if level < last:
            ylow[level, :, lane(z, span)] = solved.astype(jnp.bfloat16)
            for step in range(1, nz):
                y_copy(level, step).start()
            if level > 0:
                some = yfull.at[:, pl.ds((level - 1) * blk, blk)]
                all_in(some, yf_r.at[level - 1])
                value = dot(yfull[:, : level * blk], own[level + 1, :, : level * blk], NT)
                fpart[level + 1] = value.astype(jnp.bfloat16)
                f_far(level + 1, True)
            if level < last - 1:
                y_far(level, True)
            if level + 3 < LEVELS:
                spread(level + 3)
            if level == 0:
                load_start(2)
            relay(level + 1)
            if level > 0:
                for step in range(1, nz):
                    y_copy(level - 1, step).wait_send()
                y_far(level - 1, False)
                spread_sent(level - 1)
            if level > 1:
                f_far(level, False)

    def part_copy(level, step):
        to = (z + step) % nz
        return remote(
            part.at[level, :, lane(to, span)], sums.at[level, step - 1],
            p_s.at[level, step], p_r.at[level, step], (to, c),
        )

    for level in reversed(range(LEVELS)):
        if level < last:
            part[level] = dot(xlow[level + 1], near[level + 1], NN).astype(jnp.bfloat16)
            for step in range(1, nz):
                part_copy(level, step).start()
            if level < last - 1:
                all_in(xfull.at[level + 2], xf_r.at[level + 2])
                value = None
                for up in range(level + 2, LEVELS):
                    term = dot(xfull[up], own[up, :, level * blk : (level + 1) * blk], NN)
                    value = term if value is None else value + term
                bpart[level] = value.astype(jnp.bfloat16)
                b_far(level, True)
            if level > 0:
                x_far(level + 1, True)
            if level % 2 == 1:
                out_far(level + 1, True)
            if level == last - 1:
                for step in range(1, nz):
                    y_copy(last - 1, step).wait_send()
                f_far(last, False)
                spread_sent(last - 1)
                spread_sent(last)

                @pl.when(owner)
                def _():
                    for cut in range(len(cuts)):
                        for step in range(1, nc):
                            load_copy(cut, step).wait_send()
            else:
                for step in range(1, nz):
                    part_copy(level + 1, step).wait_send()
                x_far(level + 2, False)
            if level % 2 == 0 and level < last - 1:
                out_far(level + 2, False)
                pair = landed.at[pl.ds(level + 2, 2)]
                all_in(pair, out_r.at[level + 2])
                out[level + 2 : level + 4] = landed[level + 2 : level + 4]
            if level < last - 2:
                b_far(level + 1, False)
            for step in range(1, nz):
                part_copy(level, step).wait_recv()
        resid = yval[level]
        if level < last:
            resid = resid - part[level, :, lane(z, span)].astype(jnp.float32)
            for step in range(1, nz):
                resid = resid - sums[level, step - 1].astype(jnp.float32)
        if level < last - 1:
            all_in(bsum.at[level], b_r.at[level])
            for step in range(nz):
                resid = resid - bsum[level, step].astype(jnp.float32)
        solved = jnp.concatenate(solve(level, resid, NN), axis=1)
        xlow[level] = solved.astype(jnp.bfloat16)

    out_far(0, True)
    for step in range(1, nz):
        part_copy(0, step).wait_send()
    b_far(0, False)
    out_far(0, False)
    all_in(landed.at[pl.ds(0, 2)], out_r.at[0])
    out[0:2] = landed[0:2]


def split_plan(factor, pattern, loads, block_inverse):
    nz, nc = lax.axis_size("row"), lax.axis_size("col")
    rows, cols, blk = factor.shape[0], factor.shape[2], factor.shape[4]
    scen = loads.shape[3]
    groups, chips, width = nc // nz, nc // 2, scen // nc
    span = groups * blk
    low, f32 = jnp.bfloat16, jnp.float32
    dma = pltpu.SemaphoreType.DMA
    vmem = pl.BlockSpec(memory_space=pltpu.VMEM)
    smem = pl.BlockSpec(memory_space=pltpu.SMEM)
    result = pl.pallas_call(
        functools.partial(kernel, nz, nc, blk, scen),
        out_shape=jax.ShapeDtypeStruct((LEVELS, nc, width, blk), low),
        in_specs=[vmem, smem, vmem, vmem],
        out_specs=vmem,
        scratch_shapes=[
            pltpu.VMEM((LEVELS, scen, blk), f32),
            pltpu.VMEM((LEVELS, blk, 2 * blk), low),
            pltpu.VMEM((LEVELS, span, nc * blk), low),
            pltpu.VMEM((LEVELS, span, cols * blk), low),
            pltpu.VMEM((groups, LEVELS, width, blk), f32),
            pltpu.VMEM((groups, LEVELS, blk, 2 * blk), low),
            pltpu.VMEM((LEVELS, width, span), f32),
            pltpu.VMEM((LEVELS, width, nc * blk), low),
            pltpu.VMEM((scen, LEVELS * blk), low),
            pltpu.VMEM((LEVELS, scen, span), low),
            pltpu.VMEM((LEVELS, nc - 1, width, span), low),
            pltpu.VMEM((LEVELS, width, span), low),
            pltpu.VMEM((LEVELS, scen, span), low),
            pltpu.VMEM((LEVELS, width, nc * blk), low),
            pltpu.VMEM((LEVELS, nz - 1, width, span), low),
            pltpu.VMEM((LEVELS, scen, blk), low),
            pltpu.VMEM((LEVELS, nz, width, span), low),
            pltpu.VMEM((LEVELS, nc, width, blk), low),
            dma((LEVELS, chips)), dma((LEVELS, chips)),
            dma((LEVELS, chips)), dma((LEVELS, chips)),
            dma((3,)), dma((3, nc)), dma((3, groups)),
            dma((LEVELS,)), dma((LEVELS, chips)), dma((LEVELS, groups)),
            dma((LEVELS, groups)), dma((LEVELS, groups)),
            dma((LEVELS, nz)), dma((LEVELS, nz)),
            dma((LEVELS, nz, groups)), dma((LEVELS,)),
            dma((LEVELS, nc)), dma((LEVELS,)),
            dma((LEVELS, nz)), dma((LEVELS, nz)),
            dma((LEVELS, nc)), dma((LEVELS,)),
            dma((LEVELS, nc)), dma((LEVELS,)),
            dma((LEVELS, nz, groups)), dma((LEVELS,)),
        ],
        compiler_params=pltpu.CompilerParams(
            collective_id=0, has_side_effects=True, vmem_limit_bytes=52 * 2**20
        ),
    )(factor[:, 0, :, 0], pattern[:, 0, :, 0], loads[:, 0], block_inverse[:, 0])
    result = result.reshape(LEVELS, scen, blk).astype(f32)
    return jnp.swapaxes(result, 1, 2)[:, None]


def pick_plan(mesh):
    def plan(factor, pattern, loads, block_inverse):
        nz, nc = mesh.shape["row"], mesh.shape["col"]
        scen = loads.shape[3]
        small = nc * factor.size * 2 <= 32 * 2**20
        single = factor.shape[2] == LEVELS and factor.shape[0] == LEVELS * (nc // nz)
        even = nc % nz == 0 and nc % 2 == 0 and nz % 2 == 0 and scen % (16 * nc) == 0
        if small and even and single and loads.shape[0] == LEVELS:
            return split_plan(factor, pattern, loads, block_inverse)
        return per_device(factor, pattern, loads, block_inverse)

    return plan


def solution(mesh):
    in_specs = (
        P(None, "row", None, "col", None, None),
        P(None, "row", None, "col"),
        P(None, "col", None, None),
        P(None, "col", None, None),
    )
    out_specs = P(None, "col", None, None)
    return jax.shard_map(
        pick_plan(mesh), mesh=mesh, in_specs=in_specs, out_specs=out_specs, check_vma=False
    )
```

```python
import functools

import jax
import jax.numpy as jnp
from jax import lax
from jax.experimental import pallas as pl
from jax.experimental.pallas import tpu as pltpu
from jax.sharding import PartitionSpec as P

LEVELS = 8


def spread(value, axis, source):
    kept = jnp.where(lax.axis_index(axis) == source, value, 0).astype(value.dtype)
    return lax.psum(kept, axis)


def per_device(factor, pattern, loads, block_inverse):
    row_count = lax.axis_size("row")
    col_count = lax.axis_size("col")
    groups = col_count // row_count
    my_row = lax.axis_index("row")
    my_col = lax.axis_index("col")
    masked = factor[:, 0, :, 0] * pattern[:, 0, :, 0].astype(jnp.bfloat16)[:, :, None, None]
    per_row = factor.shape[0] // LEVELS
    per_col = factor.shape[2] // LEVELS
    rhs_local = loads[:, 0]
    inverse_local = block_inverse[:, 0]
    forward_vals = []
    forward_low = []
    for level_id in range(LEVELS):
        rhs_level = rhs_local[level_id * per_col : (level_id + 1) * per_col]
        inverse_level = inverse_local[level_id * per_col : (level_id + 1) * per_col]
        if level_id > 0:
            panel = masked[level_id * per_row : (level_id + 1) * per_row, : level_id * per_col]
            earlier = jnp.concatenate(forward_low, axis=0)
            partial_sum = jnp.einsum(
                "abpq,bqs->aps", panel, earlier, preferred_element_type=jnp.float32
            )
            row_total = lax.psum(partial_sum, "col")
            row_total = row_total.reshape((per_col, groups) + row_total.shape[1:])
            own_total = lax.dynamic_index_in_dim(
                row_total, my_col // row_count, axis=1, keepdims=False
            )
            solved = jnp.einsum(
                "mpq,mqs->mps",
                inverse_level,
                rhs_level - own_total,
                precision=lax.Precision.HIGHEST,
            )
            solved = spread(solved, "row", my_col % row_count)
        else:
            solved = jnp.einsum(
                "mpq,mqs->mps", inverse_level, rhs_level, precision=lax.Precision.HIGHEST
            )
        forward_vals.append(solved)
        forward_low.append(solved.astype(jnp.bfloat16))
    solution_parts = [None] * LEVELS
    later = []
    for level_id in reversed(range(LEVELS)):
        inverse_level = inverse_local[level_id * per_col : (level_id + 1) * per_col]
        resid = forward_vals[level_id]
        if level_id < LEVELS - 1:
            panel = masked[
                (level_id + 1) * per_row :, level_id * per_col : (level_id + 1) * per_col
            ]
            after = jnp.concatenate(later, axis=0)
            partial_sum = jnp.einsum(
                "abpq,aps->bqs", panel, after, preferred_element_type=jnp.float32
            )
            resid = resid - lax.psum(partial_sum, "row")
        solved = jnp.einsum("mqp,mqs->mps", inverse_level, resid, precision=lax.Precision.HIGHEST)
        solution_parts[level_id] = solved
        if level_id > 0:
            low_solved = solved.astype(jnp.bfloat16)
            pieces = lax.all_gather(low_solved[None], "col", axis=0, tiled=True)
            pieces = pieces.reshape((groups, row_count) + low_solved.shape)
            picked = lax.dynamic_index_in_dim(pieces, my_row, axis=1, keepdims=False)
            arranged = jnp.swapaxes(picked, 0, 1).reshape((per_row,) + low_solved.shape[1:])
            later = [arranged] + later
    solution = jnp.concatenate(solution_parts, axis=0)
    return solution[:, None]


MESH = pl.DeviceIdType.MESH
NT = (((1,), (1,)), ((), ()))
NN = (((1,), (0,)), ((), ()))


def dot(a, b, dims):
    return lax.dot_general(a, b, dims, preferred_element_type=jnp.float32)


def kernel(
    nz, nc, blk, scen, factor, pattern, loads, inverse, out,
    turned, split, near, own, rhs, diag, yval, ylow, yfull, fpart, fsum, xlow, xfull,
    part, sums, bpart, bsum, landed,
    sib_s, sib_r, chip_s, chip_r,
    load_own, load_s, load_r, diag_own, diag_s, diag_r, diag_sib_s, diag_sib_r,
    y_s, y_r, yf_s, yf_r, f_s, f_r, p_s, p_r, xf_s, xf_r, b_s, b_r, out_s, out_r,
):
    groups = nc // nz
    chips = nc // 2
    width = scen // nc
    last = LEVELS - 1
    z = lax.axis_index("row")
    c = lax.axis_index("col")
    chip = c // 2
    core = c % 2
    sibling = chip * 2 + 1 - core
    owner = c % nz == z
    relays = core == z % 2
    mine = c // nz
    span = groups * blk
    place = (c % nz) * groups + c // nz
    cuts = ((0, 1), (1, 3), (3, LEVELS))

    barrier = pltpu.get_barrier_semaphore()
    for step in range(1, nz * nc):
        other = (z * nc + c + step) % (nz * nc)
        pl.semaphore_signal(
            barrier, inc=1, device_id=(other // nc, other % nc), device_id_type=MESH
        )

    def remote(src, dst, s, r, to):
        return pltpu.make_async_remote_copy(
            src_ref=src, dst_ref=dst, send_sem=s, recv_sem=r, device_id=to, device_id_type=MESH
        )

    def share(col):
        return pl.ds(pl.multiple_of(col * width, width), width)

    def masked(row, col):
        return factor[row, col] * pattern[row, col].astype(jnp.float32).astype(jnp.bfloat16)

    def lane(index, size):
        return pl.ds(pl.multiple_of(index * size, size), size)

    def turn(level):
        turned[level] = loads[level].T

    def halves(value):
        high = value.astype(jnp.bfloat16)
        return high, (value - high.astype(jnp.float32)).astype(jnp.bfloat16)

    def prepare(level):
        high, rest = halves(inverse[level])
        split[level, :, :blk] = high
        split[level, :, blk:] = rest
        if level > 0:
            for g in range(groups):
                rows = slice(g * blk, (g + 1) * blk)
                near[level, rows, lane(place, blk)] = masked(level * groups + g, level - 1)

    prepare(0)
    turn(0)
    prepare(1)
    pl.semaphore_wait(barrier, nz * nc - 1)

    def load_copy(cut, step):
        to = (c + step) % nc
        levels = pl.ds(cuts[cut][0], cuts[cut][1] - cuts[cut][0])
        return remote(
            turned.at[levels, share(to), :], rhs.at[mine, levels],
            load_s.at[cut, step], load_r.at[cut, mine], (z, to),
        )

    def load_self(cut):
        levels = pl.ds(cuts[cut][0], cuts[cut][1] - cuts[cut][0])
        return pltpu.make_async_copy(
            turned.at[levels, share(c), :], rhs.at[mine, levels], load_own.at[cut]
        )

    def load_start(cut):
        @pl.when(owner)
        def _():
            load_self(cut).start()
            for step in range(1, nc):
                load_copy(cut, step).start()

    def load_wait(cut):
        levels = pl.ds(cuts[cut][0], cuts[cut][1] - cuts[cut][0])
        for g in range(groups):
            @pl.when(c != z + nz * g)
            def _():
                here = rhs.at[g, levels]
                remote(
                    here, here, load_s.at[cut, 0], load_r.at[cut, g], (z, sibling)
                ).wait_recv()

        @pl.when(owner)
        def _():
            load_self(cut).wait()

    def diag_copy(level, step):
        to = ((chip + step) % chips) * 2 + core
        return remote(
            split.at[level], diag.at[mine, level],
            diag_s.at[level, step], diag_r.at[level, mine], (z, to),
        )

    def diag_self(level):
        return pltpu.make_async_copy(
            split.at[level], diag.at[mine, level], diag_own.at[level]
        )

    def diag_sib(level, g):
        return remote(
            diag.at[g, level], diag.at[g, level],
            diag_sib_s.at[level, g], diag_sib_r.at[level, g], (z, sibling),
        )

    def chip_copy(level, step):
        to = ((chip + step) % chips) * 2 + core
        here = near.at[level, :, lane(place, blk)]
        return remote(here, here, chip_s.at[level, step], chip_r.at[level, step], (z, to))

    def sib_copy(level, step):
        col = ((chip + chips - step) % chips) * 2 + core
        here = near.at[level, :, lane((col % nz) * groups + col // nz, blk)]
        return remote(here, here, sib_s.at[level, step], sib_r.at[level, step], (z, sibling))

    def spread(level):
        @pl.when(owner)
        def _():
            diag_self(level).start()
            for step in range(1, chips):
                diag_copy(level, step).start()

        if level > 0:
            for step in range(1, chips):
                chip_copy(level, step).start()
            sib_copy(level, 0).start()

    load_start(0)
    spread(0)
    spread(1)
    for level in range(1, LEVELS):
        turn(level)
    load_start(1)
    prepare(2)
    spread(2)
    for level in range(3, LEVELS):
        prepare(level)
    for level in range(2, LEVELS):
        for g in range(groups):
            for col in range(level - 1):
                block = masked(level * groups + g, col)
                own[level, g * blk : (g + 1) * blk, col * blk : (col + 1) * blk] = block

    def relay(level):
        @pl.when(relays)
        def _():
            for g in range(groups):
                @pl.when(c == z + nz * g)
                def _():
                    diag_self(level).wait()

                @pl.when(c != z + nz * g)
                def _():
                    remote(
                        diag.at[g, level], diag.at[g, level], diag_s.at[level, 0],
                        diag_r.at[level, g], (z, sibling),
                    ).wait_recv()

                diag_sib(level, g).start()

        if level > 0:
            for step in range(1, chips):
                chip_copy(level, step).wait_recv()
                sib_copy(level, step).start()

    def arrived(level):
        @pl.when(jnp.logical_not(relays))
        def _():
            for g in range(groups):
                diag_sib(level, g).wait_recv()

        if level > 0:
            for step in range(chips):
                sib_copy(level, step).wait_recv()

    def spread_sent(level):
        @pl.when(owner)
        def _():
            for step in range(1, chips):
                diag_copy(level, step).wait_send()

        @pl.when(relays)
        def _():
            for g in range(groups):
                diag_sib(level, g).wait_send()

        if level > 0:
            for step in range(1, chips):
                chip_copy(level, step).wait_send()
            for step in range(chips):
                sib_copy(level, step).wait_send()

    def y_copy(level, step):
        here = ylow.at[level, :, lane(z, span)]
        return remote(
            here, here, y_s.at[level, step], y_r.at[level, step], ((z + step) % nz, c)
        )

    def to_columns(source, dst, s, r, act):
        for g in range(groups):
            src = source(g)

            for step in range(nz):
                def go():
                    copy = remote(
                        src, dst, s.at[step, g], r, ((z + step) % nz, z + nz * g)
                    )
                    copy.start() if act else copy.wait_send()

                if step > 0:
                    go()
                else:
                    pl.when(c != z + nz * g)(go)
                    if act:
                        @pl.when(c == z + nz * g)
                        def _():
                            pltpu.make_async_copy(src, dst, r).start()

    def y_far(level, act):
        here = yfull.at[share(c), pl.ds(level * blk, blk)]
        for step in range(nc):
            to = (c + step) % nc
            src = ylow.at[level, :, lane((to % nz) * groups + to // nz, blk)]
            if step > 0:
                copy = remote(src, here, yf_s.at[level, step], yf_r.at[level], (z, to))
                copy.start() if act else copy.wait_send()
            elif act:
                pltpu.make_async_copy(src, here, yf_r.at[level]).start()

    def out_far(level, act):
        pair = pl.ds(level, 2)
        to_columns(
            lambda g: xlow.at[pair, :, pl.ds(g * blk, blk)], landed.at[pair, c],
            out_s.at[level], out_r.at[level], act,
        )

    def f_far(level, act):
        for step in range(1, nc):
            to = (c + step) % nc
            copy = remote(
                fpart.at[level, share(to), :], fsum.at[level, step - 1],
                f_s.at[level, step], f_r.at[level], (z, to),
            )
            copy.start() if act else copy.wait_send()

    def x_far(level, act):
        here = xfull.at[level, share(c), :]
        for step in range(1, nc):
            copy = remote(
                xlow.at[level], here, xf_s.at[level, step], xf_r.at[level], (z, (c + step) % nc)
            )
            copy.start() if act else copy.wait_send()
        if act:
            pltpu.make_async_copy(xlow.at[level], here, xf_r.at[level]).start()

    def b_far(level, act):
        here = bsum.at[level, :, lane(place, blk)]
        for step in range(nc):
            to = (c + step) % nc
            src = bpart.at[level, share(to), :]
            if step > 0:
                copy = remote(src, here, b_s.at[level, step], b_r.at[level], (z, to))
                copy.start() if act else copy.wait_send()
            elif act:
                pltpu.make_async_copy(src, here, b_r.at[level]).start()

    def all_in(ref, sem):
        pltpu.make_async_copy(ref, ref, sem).wait()

    def apply(value, low, rest, dims):
        axis = dims[0][1][0]
        high, small = halves(value)
        left = jnp.concatenate([high, small, high], axis=1)
        return dot(left, jnp.concatenate([low, low, rest], axis=axis), dims)

    def solve(level, value, dims):
        return [
            apply(
                value[:, g * blk : (g + 1) * blk],
                diag[g, level, :, :blk], diag[g, level, :, blk:], dims,
            )
            for g in range(groups)
        ]

    relay(0)
    load_wait(0)

    for level in range(LEVELS):
        for cut in range(1, len(cuts)):
            if level == cuts[cut][0]:
                load_wait(cut)
        arrived(level)
        resid = jnp.concatenate([rhs[g, level] for g in range(groups)], axis=1)
        if level > 0:
            for step in range(1, nz):
                y_copy(level - 1, step).wait_recv()
            if level < last:
                y_far(level - 1, True)
            resid = resid - dot(ylow[level - 1], near[level], NT)
        if level > 1:
            resid = resid - fpart[level, share(c), :].astype(jnp.float32)
            all_in(fsum.at[level], f_r.at[level])
            for step in range(nc - 1):
                resid = resid - fsum[level, step].astype(jnp.float32)
        solved = jnp.concatenate(solve(level, resid, NT), axis=1)
        yval[level] = solved
        if level < last:
            ylow[level, :, lane(z, span)] = solved.astype(jnp.bfloat16)
            for step in range(1, nz):
                y_copy(level, step).start()
            if level > 0:
                value = None
                if level > 1:
                    done = slice(0, (level - 1) * blk)
                    value = dot(yfull[:, done], own[level + 1, :, done], NT)
                fresh = slice((level - 1) * blk, level * blk)
                all_in(yfull.at[:, pl.ds((level - 1) * blk, blk)], yf_r.at[level - 1])
                term = dot(yfull[:, fresh], own[level + 1, :, fresh], NT)
                value = term if value is None else value + term
                fpart[level + 1] = value.astype(jnp.bfloat16)
                f_far(level + 1, True)
            if level + 3 < LEVELS:
                spread(level + 3)
            if level == 0:
                load_start(2)
            relay(level + 1)
            if level > 0:
                for step in range(1, nz):
                    y_copy(level - 1, step).wait_send()
                y_far(level - 1, False)
                spread_sent(level - 1)
            if level > 1:
                f_far(level, False)

    def part_copy(level, step):
        to = (z + step) % nz
        return remote(
            part.at[level, :, lane(to, span)], sums.at[level, step - 1],
            p_s.at[level, step], p_r.at[level, step], (to, c),
        )

    for level in reversed(range(LEVELS)):
        if level < last:
            value = dot(xlow[level + 1], near[level + 1], NN)
            if level < last - 1:
                all_in(bsum.at[level], b_r.at[level])
                value = value + bsum[level].astype(jnp.float32)
            part[level] = value.astype(jnp.bfloat16)
            for step in range(1, nz):
                part_copy(level, step).start()
            if level > 0:
                x_far(level + 1, True)
            if level % 2 == 1:
                out_far(level + 1, True)
            if level == last - 1:
                for step in range(1, nz):
                    y_copy(last - 1, step).wait_send()
                f_far(last, False)
                spread_sent(last - 1)
                spread_sent(last)

                @pl.when(owner)
                def _():
                    for cut in range(len(cuts)):
                        for step in range(1, nc):
                            load_copy(cut, step).wait_send()
            else:
                for step in range(1, nz):
                    part_copy(level + 1, step).wait_send()
                x_far(level + 2, False)
            if level % 2 == 0 and level < last - 1:
                out_far(level + 2, False)
                pair = landed.at[pl.ds(level + 2, 2)]
                all_in(pair, out_r.at[level + 2])
                out[level + 2 : level + 4] = landed[level + 2 : level + 4]
            if level > 0:
                value = None
                lanes = slice((level - 1) * blk, level * blk)
                for up in reversed(range(level + 1, LEVELS)):
                    if up == level + 1:
                        all_in(xfull.at[up], xf_r.at[up])
                    term = dot(xfull[up], own[up, :, lanes], NN)
                    value = term if value is None else value + term
                bpart[level - 1] = value.astype(jnp.bfloat16)
                b_far(level - 1, True)
            if level < last - 1:
                b_far(level, False)
            for step in range(1, nz):
                part_copy(level, step).wait_recv()
        resid = yval[level]
        if level < last:
            resid = resid - part[level, :, lane(z, span)].astype(jnp.float32)
            for step in range(1, nz):
                resid = resid - sums[level, step - 1].astype(jnp.float32)
        solved = jnp.concatenate(solve(level, resid, NN), axis=1)
        xlow[level] = solved.astype(jnp.bfloat16)

    out_far(0, True)
    for step in range(1, nz):
        part_copy(0, step).wait_send()
    out_far(0, False)
    all_in(landed.at[pl.ds(0, 2)], out_r.at[0])
    out[0:2] = landed[0:2]


def split_plan(factor, pattern, loads, block_inverse):
    nz, nc = lax.axis_size("row"), lax.axis_size("col")
    rows, cols, blk = factor.shape[0], factor.shape[2], factor.shape[4]
    scen = loads.shape[3]
    groups, chips, width = nc // nz, nc // 2, scen // nc
    span = groups * blk
    low, f32 = jnp.bfloat16, jnp.float32
    dma = pltpu.SemaphoreType.DMA
    vmem = pl.BlockSpec(memory_space=pltpu.VMEM)
    smem = pl.BlockSpec(memory_space=pltpu.SMEM)
    result = pl.pallas_call(
        functools.partial(kernel, nz, nc, blk, scen),
        out_shape=jax.ShapeDtypeStruct((LEVELS, nc, width, blk), low),
        in_specs=[vmem, smem, vmem, vmem],
        out_specs=vmem,
        scratch_shapes=[
            pltpu.VMEM((LEVELS, scen, blk), f32),
            pltpu.VMEM((LEVELS, blk, 2 * blk), low),
            pltpu.VMEM((LEVELS, span, nc * blk), low),
            pltpu.VMEM((LEVELS, span, cols * blk), low),
            pltpu.VMEM((groups, LEVELS, width, blk), f32),
            pltpu.VMEM((groups, LEVELS, blk, 2 * blk), low),
            pltpu.VMEM((LEVELS, width, span), f32),
            pltpu.VMEM((LEVELS, width, nc * blk), low),
            pltpu.VMEM((scen, LEVELS * blk), low),
            pltpu.VMEM((LEVELS, scen, span), low),
            pltpu.VMEM((LEVELS, nc - 1, width, span), low),
            pltpu.VMEM((LEVELS, width, span), low),
            pltpu.VMEM((LEVELS, scen, span), low),
            pltpu.VMEM((LEVELS, width, nc * blk), low),
            pltpu.VMEM((LEVELS, nz - 1, width, span), low),
            pltpu.VMEM((LEVELS, scen, blk), low),
            pltpu.VMEM((LEVELS, width, nc * blk), low),
            pltpu.VMEM((LEVELS, nc, width, blk), low),
            dma((LEVELS, chips)), dma((LEVELS, chips)),
            dma((LEVELS, chips)), dma((LEVELS, chips)),
            dma((3,)), dma((3, nc)), dma((3, groups)),
            dma((LEVELS,)), dma((LEVELS, chips)), dma((LEVELS, groups)),
            dma((LEVELS, groups)), dma((LEVELS, groups)),
            dma((LEVELS, nz)), dma((LEVELS, nz)),
            dma((LEVELS, nc)), dma((LEVELS,)),
            dma((LEVELS, nc)), dma((LEVELS,)),
            dma((LEVELS, nz)), dma((LEVELS, nz)),
            dma((LEVELS, nc)), dma((LEVELS,)),
            dma((LEVELS, nc)), dma((LEVELS,)),
            dma((LEVELS, nz, groups)), dma((LEVELS,)),
        ],
        compiler_params=pltpu.CompilerParams(
            collective_id=0, has_side_effects=True, vmem_limit_bytes=52 * 2**20
        ),
    )(factor[:, 0, :, 0], pattern[:, 0, :, 0], loads[:, 0], block_inverse[:, 0])
    result = result.reshape(LEVELS, scen, blk).astype(f32)
    return jnp.swapaxes(result, 1, 2)[:, None]


def pick_plan(mesh):
    def plan(factor, pattern, loads, block_inverse):
        nz, nc = mesh.shape["row"], mesh.shape["col"]
        scen = loads.shape[3]
        small = nc * factor.size * 2 <= 32 * 2**20
        single = factor.shape[2] == LEVELS and factor.shape[0] == LEVELS * (nc // nz)
        even = nc % nz == 0 and nc % 2 == 0 and nz % 2 == 0 and scen % (16 * nc) == 0
        if small and even and single and loads.shape[0] == LEVELS:
            return split_plan(factor, pattern, loads, block_inverse)
        return per_device(factor, pattern, loads, block_inverse)

    return plan


def solution(mesh):
    in_specs = (
        P(None, "row", None, "col", None, None),
        P(None, "row", None, "col"),
        P(None, "col", None, None),
        P(None, "col", None, None),
    )
    out_specs = P(None, "col", None, None)
    return jax.shard_map(
        pick_plan(mesh), mesh=mesh, in_specs=in_specs, out_specs=out_specs, check_vma=False
    )
```

```python
import functools

import jax
import jax.numpy as jnp
from jax import lax
from jax.experimental import pallas as pl
from jax.experimental.pallas import tpu as pltpu
from jax.sharding import PartitionSpec as P

LEVELS = 8


def spread(value, axis, source):
    kept = jnp.where(lax.axis_index(axis) == source, value, 0).astype(value.dtype)
    return lax.psum(kept, axis)


def per_device(factor, pattern, loads, block_inverse):
    row_count = lax.axis_size("row")
    col_count = lax.axis_size("col")
    groups = col_count // row_count
    my_row = lax.axis_index("row")
    my_col = lax.axis_index("col")
    masked = factor[:, 0, :, 0] * pattern[:, 0, :, 0].astype(jnp.bfloat16)[:, :, None, None]
    per_row = factor.shape[0] // LEVELS
    per_col = factor.shape[2] // LEVELS
    rhs_local = loads[:, 0]
    inverse_local = block_inverse[:, 0]
    forward_vals = []
    forward_low = []
    for level_id in range(LEVELS):
        rhs_level = rhs_local[level_id * per_col : (level_id + 1) * per_col]
        inverse_level = inverse_local[level_id * per_col : (level_id + 1) * per_col]
        if level_id > 0:
            panel = masked[level_id * per_row : (level_id + 1) * per_row, : level_id * per_col]
            earlier = jnp.concatenate(forward_low, axis=0)
            partial_sum = jnp.einsum(
                "abpq,bqs->aps", panel, earlier, preferred_element_type=jnp.float32
            )
            row_total = lax.psum(partial_sum, "col")
            row_total = row_total.reshape((per_col, groups) + row_total.shape[1:])
            own_total = lax.dynamic_index_in_dim(
                row_total, my_col // row_count, axis=1, keepdims=False
            )
            solved = jnp.einsum(
                "mpq,mqs->mps",
                inverse_level,
                rhs_level - own_total,
                precision=lax.Precision.HIGHEST,
            )
            solved = spread(solved, "row", my_col % row_count)
        else:
            solved = jnp.einsum(
                "mpq,mqs->mps", inverse_level, rhs_level, precision=lax.Precision.HIGHEST
            )
        forward_vals.append(solved)
        forward_low.append(solved.astype(jnp.bfloat16))
    solution_parts = [None] * LEVELS
    later = []
    for level_id in reversed(range(LEVELS)):
        inverse_level = inverse_local[level_id * per_col : (level_id + 1) * per_col]
        resid = forward_vals[level_id]
        if level_id < LEVELS - 1:
            panel = masked[
                (level_id + 1) * per_row :, level_id * per_col : (level_id + 1) * per_col
            ]
            after = jnp.concatenate(later, axis=0)
            partial_sum = jnp.einsum(
                "abpq,aps->bqs", panel, after, preferred_element_type=jnp.float32
            )
            resid = resid - lax.psum(partial_sum, "row")
        solved = jnp.einsum("mqp,mqs->mps", inverse_level, resid, precision=lax.Precision.HIGHEST)
        solution_parts[level_id] = solved
        if level_id > 0:
            low_solved = solved.astype(jnp.bfloat16)
            pieces = lax.all_gather(low_solved[None], "col", axis=0, tiled=True)
            pieces = pieces.reshape((groups, row_count) + low_solved.shape)
            picked = lax.dynamic_index_in_dim(pieces, my_row, axis=1, keepdims=False)
            arranged = jnp.swapaxes(picked, 0, 1).reshape((per_row,) + low_solved.shape[1:])
            later = [arranged] + later
    solution = jnp.concatenate(solution_parts, axis=0)
    return solution[:, None]


MESH = pl.DeviceIdType.MESH
NT = (((1,), (1,)), ((), ()))
NN = (((1,), (0,)), ((), ()))


def dot(a, b, dims):
    return lax.dot_general(a, b, dims, preferred_element_type=jnp.float32)


def kernel(
    nz, nc, blk, scen, factor, pattern, loads, inverse, out,
    turned, split, near, own, rhs, diag, yval, ylow, yfull, fpart, fsum, xlow, xfull,
    part, sums, bpart, bsum, landed,
    sib_s, sib_r, chip_s, chip_r,
    load_own, load_s, load_r, diag_own, diag_s, diag_r, diag_sib_s, diag_sib_r,
    y_s, y_r, yf_s, yf_r, f_s, f_r, p_s, p_r, xf_s, xf_r, b_s, b_r, out_s, out_r,
):
    groups = nc // nz
    chips = nc // 2
    width = scen // nc
    last = LEVELS - 1
    z = lax.axis_index("row")
    c = lax.axis_index("col")
    chip = c // 2
    core = c % 2
    sibling = chip * 2 + 1 - core
    owner = c % nz == z
    relays = core == z % 2
    mine = c // nz
    span = groups * blk
    place = (c % nz) * groups + c // nz
    cuts = ((0, 1), (1, 3), (3, LEVELS))

    barrier = pltpu.get_barrier_semaphore()
    for step in range(1, nz * nc):
        other = (z * nc + c + step) % (nz * nc)
        pl.semaphore_signal(
            barrier, inc=1, device_id=(other // nc, other % nc), device_id_type=MESH
        )

    def remote(src, dst, s, r, to):
        return pltpu.make_async_remote_copy(
            src_ref=src, dst_ref=dst, send_sem=s, recv_sem=r, device_id=to, device_id_type=MESH
        )

    def share(col):
        return pl.ds(pl.multiple_of(col * width, width), width)

    def masked(row, col):
        return factor[row, col] * pattern[row, col].astype(jnp.float32).astype(jnp.bfloat16)

    def lane(index, size):
        return pl.ds(pl.multiple_of(index * size, size), size)

    def turn(level):
        turned[level] = loads[level].T

    def halves(value):
        high = value.astype(jnp.bfloat16)
        return high, (value - high.astype(jnp.float32)).astype(jnp.bfloat16)

    def prepare(level):
        high, rest = halves(inverse[level])
        split[level, :, :blk] = high
        split[level, :, blk:] = rest
        if level > 0:
            for g in range(groups):
                rows = slice(g * blk, (g + 1) * blk)
                near[level, rows, lane(place, blk)] = masked(level * groups + g, level - 1)

    prepare(0)
    turn(0)
    prepare(1)
    pl.semaphore_wait(barrier, nz * nc - 1)

    def load_copy(cut, step):
        to = (c + step) % nc
        levels = pl.ds(cuts[cut][0], cuts[cut][1] - cuts[cut][0])
        return remote(
            turned.at[levels, share(to), :], rhs.at[mine, levels],
            load_s.at[cut, step], load_r.at[cut, mine], (z, to),
        )

    def load_self(cut):
        levels = pl.ds(cuts[cut][0], cuts[cut][1] - cuts[cut][0])
        return pltpu.make_async_copy(
            turned.at[levels, share(c), :], rhs.at[mine, levels], load_own.at[cut]
        )

    def load_start(cut):
        @pl.when(owner)
        def _():
            load_self(cut).start()
            for step in range(1, nc):
                load_copy(cut, step).start()

    def load_wait(cut):
        levels = pl.ds(cuts[cut][0], cuts[cut][1] - cuts[cut][0])
        for g in range(groups):
            @pl.when(c != z + nz * g)
            def _():
                here = rhs.at[g, levels]
                remote(
                    here, here, load_s.at[cut, 0], load_r.at[cut, g], (z, sibling)
                ).wait_recv()

        @pl.when(owner)
        def _():
            load_self(cut).wait()

    def diag_copy(level, step):
        to = ((chip + step) % chips) * 2 + core
        return remote(
            split.at[level], diag.at[mine, level],
            diag_s.at[level, step], diag_r.at[level, mine], (z, to),
        )

    def diag_self(level):
        return pltpu.make_async_copy(
            split.at[level], diag.at[mine, level], diag_own.at[level]
        )

    def diag_sib(level, g):
        return remote(
            diag.at[g, level], diag.at[g, level],
            diag_sib_s.at[level, g], diag_sib_r.at[level, g], (z, sibling),
        )

    def chip_copy(level, step):
        to = ((chip + step) % chips) * 2 + core
        here = near.at[level, :, lane(place, blk)]
        return remote(here, here, chip_s.at[level, step], chip_r.at[level, step], (z, to))

    def sib_copy(level, step):
        col = ((chip + chips - step) % chips) * 2 + core
        here = near.at[level, :, lane((col % nz) * groups + col // nz, blk)]
        return remote(here, here, sib_s.at[level, step], sib_r.at[level, step], (z, sibling))

    def spread(level):
        @pl.when(owner)
        def _():
            diag_self(level).start()
            for step in range(1, chips):
                diag_copy(level, step).start()

        if level > 0:
            for step in range(1, chips):
                chip_copy(level, step).start()
            sib_copy(level, 0).start()

    load_start(0)
    spread(0)
    spread(1)
    for level in range(1, LEVELS):
        turn(level)
    load_start(1)
    prepare(2)
    spread(2)
    for level in range(3, LEVELS):
        prepare(level)
    for level in range(2, LEVELS):
        for g in range(groups):
            for col in range(level - 1):
                block = masked(level * groups + g, col)
                own[level, g * blk : (g + 1) * blk, col * blk : (col + 1) * blk] = block

    def relay(level):
        @pl.when(relays)
        def _():
            for g in range(groups):
                @pl.when(c == z + nz * g)
                def _():
                    diag_self(level).wait()

                @pl.when(c != z + nz * g)
                def _():
                    remote(
                        diag.at[g, level], diag.at[g, level], diag_s.at[level, 0],
                        diag_r.at[level, g], (z, sibling),
                    ).wait_recv()

                diag_sib(level, g).start()

        if level > 0:
            for step in range(1, chips):
                chip_copy(level, step).wait_recv()
                sib_copy(level, step).start()

    def arrived(level):
        @pl.when(jnp.logical_not(relays))
        def _():
            for g in range(groups):
                diag_sib(level, g).wait_recv()

        if level > 0:
            for step in range(chips):
                sib_copy(level, step).wait_recv()

    def spread_sent(level):
        @pl.when(owner)
        def _():
            for step in range(1, chips):
                diag_copy(level, step).wait_send()

        @pl.when(relays)
        def _():
            for g in range(groups):
                diag_sib(level, g).wait_send()

        if level > 0:
            for step in range(1, chips):
                chip_copy(level, step).wait_send()
            for step in range(chips):
                sib_copy(level, step).wait_send()

    def y_copy(level, step):
        here = ylow.at[level, :, lane(z, span)]
        return remote(
            here, here, y_s.at[level, step], y_r.at[level, step], ((z + step) % nz, c)
        )

    def to_columns(source, dst, s, r, act):
        for g in range(groups):
            src = source(g)

            for step in range(nz):
                def go():
                    copy = remote(
                        src, dst, s.at[step, g], r, ((z + step) % nz, z + nz * g)
                    )
                    copy.start() if act else copy.wait_send()

                if step > 0:
                    go()
                else:
                    pl.when(c != z + nz * g)(go)
                    if act:
                        @pl.when(c == z + nz * g)
                        def _():
                            pltpu.make_async_copy(src, dst, r).start()

    def y_far(level, act):
        to_columns(
            lambda g: ylow.at[level, :, lane(z * groups + g, blk)],
            yfull.at[share(c), pl.ds(level * blk, blk)],
            yf_s.at[level], yf_r.at[level], act,
        )

    def out_far(level, act):
        pair = pl.ds(level, 2)
        to_columns(
            lambda g: xlow.at[pair, :, pl.ds(g * blk, blk)], landed.at[pair, c],
            out_s.at[level], out_r.at[level], act,
        )

    def f_far(level, act):
        for step in range(1, nc):
            to = (c + step) % nc
            copy = remote(
                fpart.at[level, share(to), :], fsum.at[level, step - 1],
                f_s.at[level, step], f_r.at[level], (z, to),
            )
            copy.start() if act else copy.wait_send()

    def x_far(level, act):
        here = xfull.at[level, share(c), :]
        for step in range(1, nc):
            copy = remote(
                xlow.at[level], here, xf_s.at[level, step], xf_r.at[level], (z, (c + step) % nc)
            )
            copy.start() if act else copy.wait_send()
        if act:
            pltpu.make_async_copy(xlow.at[level], here, xf_r.at[level]).start()

    def b_far(level, act):
        for step in range(nc):
            to = (c + step) % nc
            src, dst = bpart.at[level, share(to), :], bsum.at[level, z, :, lane(mine, blk)]

            def go():
                copy = remote(src, dst, b_s.at[level, step], b_r.at[level], (c % nz, to))
                copy.start() if act else copy.wait_send()

            if step > 0:
                go()
            else:
                pl.when(jnp.logical_not(owner))(go)
                if act:
                    @pl.when(owner)
                    def _():
                        pltpu.make_async_copy(src, dst, b_r.at[level]).start()

    def all_in(ref, sem):
        pltpu.make_async_copy(ref, ref, sem).wait()

    def apply(value, low, rest, dims):
        axis = dims[0][1][0]
        high, small = halves(value)
        left = jnp.concatenate([high, small, high], axis=1)
        return dot(left, jnp.concatenate([low, low, rest], axis=axis), dims)

    def solve(level, value, dims):
        return [
            apply(
                value[:, g * blk : (g + 1) * blk],
                diag[g, level, :, :blk], diag[g, level, :, blk:], dims,
            )
            for g in range(groups)
        ]

    relay(0)
    load_wait(0)

    for level in range(LEVELS):
        for cut in range(1, len(cuts)):
            if level == cuts[cut][0]:
                load_wait(cut)
        arrived(level)
        resid = jnp.concatenate([rhs[g, level] for g in range(groups)], axis=1)
        if level > 0:
            for step in range(1, nz):
                y_copy(level - 1, step).wait_recv()
            resid = resid - dot(ylow[level - 1], near[level], NT)
        if level > 1:
            resid = resid - fpart[level, share(c), :].astype(jnp.float32)
            all_in(fsum.at[level], f_r.at[level])
            for step in range(nc - 1):
                resid = resid - fsum[level, step].astype(jnp.float32)
        solved = jnp.concatenate(solve(level, resid, NT), axis=1)
        yval[level] = solved
        if level < last:
            ylow[level, :, lane(z, span)] = solved.astype(jnp.bfloat16)
            for step in range(1, nz):
                y_copy(level, step).start()
            if level < last - 1:
                y_far(level, True)
            if level > 0:
                value = None
                if level > 1:
                    done = slice(0, (level - 1) * blk)
                    value = dot(yfull[:, done], own[level + 1, :, done], NT)
                fresh = slice((level - 1) * blk, level * blk)
                all_in(yfull.at[:, pl.ds((level - 1) * blk, blk)], yf_r.at[level - 1])
                term = dot(yfull[:, fresh], own[level + 1, :, fresh], NT)
                value = term if value is None else value + term
                fpart[level + 1] = value.astype(jnp.bfloat16)
                f_far(level + 1, True)
            if level + 3 < LEVELS:
                spread(level + 3)
            if level == 0:
                load_start(2)
            relay(level + 1)

    def part_copy(level, step):
        to = (z + step) % nz
        return remote(
            part.at[level, :, lane(to, span)], sums.at[level, step - 1],
            p_s.at[level, step], p_r.at[level, step], (to, c),
        )

    for level in reversed(range(LEVELS)):
        if level < last:
            value = dot(xlow[level + 1], near[level + 1], NN)
            part[level] = value.astype(jnp.bfloat16)
            for step in range(1, nz):
                part_copy(level, step).start()
            if level > 0:
                x_far(level + 1, True)
                value = None
                lanes = slice((level - 1) * blk, level * blk)
                for up in reversed(range(level + 1, LEVELS)):
                    if up == level + 1:
                        all_in(xfull.at[up], xf_r.at[up])
                    term = dot(xfull[up], own[up, :, lanes], NN)
                    value = term if value is None else value + term
                bpart[level - 1] = value.astype(jnp.bfloat16)
                b_far(level - 1, True)
            if level % 2 == 1:
                out_far(level + 1, True)
        resid = yval[level]
        if level < last:
            resid = resid - part[level, :, lane(z, span)].astype(jnp.float32)
        if level < last - 1:
            all_in(bsum.at[level], b_r.at[level])
            for step in range(nz):
                resid = resid - bsum[level, step].astype(jnp.float32)
        if level < last:
            for step in range(1, nz):
                part_copy(level, step).wait_recv()
                resid = resid - sums[level, step - 1].astype(jnp.float32)
        solved = jnp.concatenate(solve(level, resid, NN), axis=1)
        xlow[level] = solved.astype(jnp.bfloat16)

    out_far(0, True)
    for level in range(last):
        for step in range(1, nz):
            y_copy(level, step).wait_send()
            part_copy(level, step).wait_send()
        if level < last - 1:
            y_far(level, False)
            b_far(level, False)
            f_far(level + 2, False)
            x_far(level + 2, False)
    for level in range(LEVELS):
        spread_sent(level)

    @pl.when(owner)
    def _():
        for cut in range(len(cuts)):
            for step in range(1, nc):
                load_copy(cut, step).wait_send()

    for level in reversed(range(0, LEVELS, 2)):
        out_far(level, False)
        all_in(landed.at[pl.ds(level, 2)], out_r.at[level])
        out[level : level + 2] = landed[level : level + 2]


def split_plan(factor, pattern, loads, block_inverse):
    nz, nc = lax.axis_size("row"), lax.axis_size("col")
    rows, cols, blk = factor.shape[0], factor.shape[2], factor.shape[4]
    scen = loads.shape[3]
    groups, chips, width = nc // nz, nc // 2, scen // nc
    span = groups * blk
    low, f32 = jnp.bfloat16, jnp.float32
    dma = pltpu.SemaphoreType.DMA
    vmem = pl.BlockSpec(memory_space=pltpu.VMEM)
    smem = pl.BlockSpec(memory_space=pltpu.SMEM)
    result = pl.pallas_call(
        functools.partial(kernel, nz, nc, blk, scen),
        out_shape=jax.ShapeDtypeStruct((LEVELS, nc, width, blk), low),
        in_specs=[vmem, smem, vmem, vmem],
        out_specs=vmem,
        scratch_shapes=[
            pltpu.VMEM((LEVELS, scen, blk), f32),
            pltpu.VMEM((LEVELS, blk, 2 * blk), low),
            pltpu.VMEM((LEVELS, span, nc * blk), low),
            pltpu.VMEM((LEVELS, span, cols * blk), low),
            pltpu.VMEM((groups, LEVELS, width, blk), f32),
            pltpu.VMEM((groups, LEVELS, blk, 2 * blk), low),
            pltpu.VMEM((LEVELS, width, span), f32),
            pltpu.VMEM((LEVELS, width, nc * blk), low),
            pltpu.VMEM((scen, LEVELS * blk), low),
            pltpu.VMEM((LEVELS, scen, span), low),
            pltpu.VMEM((LEVELS, nc - 1, width, span), low),
            pltpu.VMEM((LEVELS, width, span), low),
            pltpu.VMEM((LEVELS, scen, span), low),
            pltpu.VMEM((LEVELS, width, nc * blk), low),
            pltpu.VMEM((LEVELS, nz - 1, width, span), low),
            pltpu.VMEM((LEVELS, scen, blk), low),
            pltpu.VMEM((LEVELS, nz, width, span), low),
            pltpu.VMEM((LEVELS, nc, width, blk), low),
            dma((LEVELS, chips)), dma((LEVELS, chips)),
            dma((LEVELS, chips)), dma((LEVELS, chips)),
            dma((3,)), dma((3, nc)), dma((3, groups)),
            dma((LEVELS,)), dma((LEVELS, chips)), dma((LEVELS, groups)),
            dma((LEVELS, groups)), dma((LEVELS, groups)),
            dma((LEVELS, nz)), dma((LEVELS, nz)),
            dma((LEVELS, nz, groups)), dma((LEVELS,)),
            dma((LEVELS, nc)), dma((LEVELS,)),
            dma((LEVELS, nz)), dma((LEVELS, nz)),
            dma((LEVELS, nc)), dma((LEVELS,)),
            dma((LEVELS, nc)), dma((LEVELS,)),
            dma((LEVELS, nz, groups)), dma((LEVELS,)),
        ],
        compiler_params=pltpu.CompilerParams(
            collective_id=0, has_side_effects=True, vmem_limit_bytes=52 * 2**20
        ),
    )(factor[:, 0, :, 0], pattern[:, 0, :, 0], loads[:, 0], block_inverse[:, 0])
    result = result.reshape(LEVELS, scen, blk).astype(f32)
    return jnp.swapaxes(result, 1, 2)[:, None]


def pick_plan(mesh):
    def plan(factor, pattern, loads, block_inverse):
        nz, nc = mesh.shape["row"], mesh.shape["col"]
        scen = loads.shape[3]
        small = nc * factor.size * 2 <= 32 * 2**20
        single = factor.shape[2] == LEVELS and factor.shape[0] == LEVELS * (nc // nz)
        even = nc % nz == 0 and nc % 2 == 0 and nz % 2 == 0 and scen % (16 * nc) == 0
        if small and even and single and loads.shape[0] == LEVELS:
            return split_plan(factor, pattern, loads, block_inverse)
        return per_device(factor, pattern, loads, block_inverse)

    return plan


def solution(mesh):
    in_specs = (
        P(None, "row", None, "col", None, None),
        P(None, "row", None, "col"),
        P(None, "col", None, None),
        P(None, "col", None, None),
    )
    out_specs = P(None, "col", None, None)
    return jax.shard_map(
        pick_plan(mesh), mesh=mesh, in_specs=in_specs, out_specs=out_specs, check_vma=False
    )
```

```python
import functools

import jax
import jax.numpy as jnp
from jax import lax
from jax.experimental import pallas as pl
from jax.experimental.pallas import tpu as pltpu
from jax.sharding import PartitionSpec as P

LEVELS = 8


def spread(value, axis, source):
    kept = jnp.where(lax.axis_index(axis) == source, value, 0).astype(value.dtype)
    return lax.psum(kept, axis)


def per_device(factor, pattern, loads, block_inverse):
    row_count = lax.axis_size("row")
    col_count = lax.axis_size("col")
    groups = col_count // row_count
    my_row = lax.axis_index("row")
    my_col = lax.axis_index("col")
    masked = factor[:, 0, :, 0] * pattern[:, 0, :, 0].astype(jnp.bfloat16)[:, :, None, None]
    per_row = factor.shape[0] // LEVELS
    per_col = factor.shape[2] // LEVELS
    rhs_local = loads[:, 0]
    inverse_local = block_inverse[:, 0]
    forward_vals = []
    forward_low = []
    for level_id in range(LEVELS):
        rhs_level = rhs_local[level_id * per_col : (level_id + 1) * per_col]
        inverse_level = inverse_local[level_id * per_col : (level_id + 1) * per_col]
        if level_id > 0:
            panel = masked[level_id * per_row : (level_id + 1) * per_row, : level_id * per_col]
            earlier = jnp.concatenate(forward_low, axis=0)
            partial_sum = jnp.einsum(
                "abpq,bqs->aps", panel, earlier, preferred_element_type=jnp.float32
            )
            row_total = lax.psum(partial_sum, "col")
            row_total = row_total.reshape((per_col, groups) + row_total.shape[1:])
            own_total = lax.dynamic_index_in_dim(
                row_total, my_col // row_count, axis=1, keepdims=False
            )
            solved = jnp.einsum(
                "mpq,mqs->mps",
                inverse_level,
                rhs_level - own_total,
                precision=lax.Precision.HIGHEST,
            )
            solved = spread(solved, "row", my_col % row_count)
        else:
            solved = jnp.einsum(
                "mpq,mqs->mps", inverse_level, rhs_level, precision=lax.Precision.HIGHEST
            )
        forward_vals.append(solved)
        forward_low.append(solved.astype(jnp.bfloat16))
    solution_parts = [None] * LEVELS
    later = []
    for level_id in reversed(range(LEVELS)):
        inverse_level = inverse_local[level_id * per_col : (level_id + 1) * per_col]
        resid = forward_vals[level_id]
        if level_id < LEVELS - 1:
            panel = masked[
                (level_id + 1) * per_row :, level_id * per_col : (level_id + 1) * per_col
            ]
            after = jnp.concatenate(later, axis=0)
            partial_sum = jnp.einsum(
                "abpq,aps->bqs", panel, after, preferred_element_type=jnp.float32
            )
            resid = resid - lax.psum(partial_sum, "row")
        solved = jnp.einsum("mqp,mqs->mps", inverse_level, resid, precision=lax.Precision.HIGHEST)
        solution_parts[level_id] = solved
        if level_id > 0:
            low_solved = solved.astype(jnp.bfloat16)
            pieces = lax.all_gather(low_solved[None], "col", axis=0, tiled=True)
            pieces = pieces.reshape((groups, row_count) + low_solved.shape)
            picked = lax.dynamic_index_in_dim(pieces, my_row, axis=1, keepdims=False)
            arranged = jnp.swapaxes(picked, 0, 1).reshape((per_row,) + low_solved.shape[1:])
            later = [arranged] + later
    solution = jnp.concatenate(solution_parts, axis=0)
    return solution[:, None]


MESH = pl.DeviceIdType.MESH
NT = (((1,), (1,)), ((), ()))
NN = (((1,), (0,)), ((), ()))


def dot(a, b, dims):
    return lax.dot_general(a, b, dims, preferred_element_type=jnp.float32)


def kernel(
    nz, nc, blk, scen, factor, pattern, loads, inverse, out,
    turned, split, near, own, rhs, diag, yval, ylow, yfull, fpart, fsum, xlow, xfull,
    part, sums, bpart, bsum, landed,
    sib_s, sib_r, chip_s, chip_r,
    load_own, load_s, load_r, diag_own, diag_s, diag_r, diag_sib_s, diag_sib_r,
    y_s, y_r, yf_s, yf_r, f_s, f_r, p_s, p_r, xf_s, xf_r, b_s, b_r, out_s, out_r,
):
    groups = nc // nz
    chips = nc // 2
    width = scen // nc
    last = LEVELS - 1
    z = lax.axis_index("row")
    c = lax.axis_index("col")
    chip = c // 2
    core = c % 2
    sibling = chip * 2 + 1 - core
    owner = c % nz == z
    leads = [c == z + nz * g for g in range(nc // nz)]
    trails = [c != z + nz * g for g in range(nc // nz)]
    relays = core == z % 2
    mine = c // nz
    span = groups * blk
    rank = (z % 2) * (nz // 2) + z // 2
    cols = [c] + [(c + step) % nc for step in range(1, nc)]
    rows_z = [z] + [(z + step) % nz for step in range(1, nz)]
    ranks = [rank] + [(to % 2) * (nz // 2) + to // 2 for to in rows_z[1:]]
    peers = [c] + [((chip + step) % chips) * 2 + core for step in range(1, chips)]
    home = c % nz
    place = ((home % 2) * (nz // 2) + home // 2) * groups + mine
    cuts = ((0, 1), (1, 3), (3, LEVELS))

    barrier = pltpu.get_barrier_semaphore()
    for step in range(1, nz * nc):
        other = (z * nc + c + step) % (nz * nc)
        pl.semaphore_signal(
            barrier, inc=1, device_id=(other // nc, other % nc), device_id_type=MESH
        )

    def remote(src, dst, s, r, to):
        return pltpu.make_async_remote_copy(
            src_ref=src, dst_ref=dst, send_sem=s, recv_sem=r, device_id=to, device_id_type=MESH
        )

    def share(col):
        return pl.ds(pl.multiple_of(col * width, width), width)

    def masked(row, col):
        return factor[row, col] * pattern[row, col].astype(jnp.float32).astype(jnp.bfloat16)

    def lane(index, size):
        return pl.ds(pl.multiple_of(index * size, size), size)

    def turn(level):
        turned[level] = loads[level].T

    def halves(value):
        high = value.astype(jnp.bfloat16)
        return high, (value - high.astype(jnp.float32)).astype(jnp.bfloat16)

    def prepare(level):
        high, rest = halves(inverse[level])
        split[level, :, :blk] = high
        split[level, :, blk:] = rest
        if level > 0:
            for g in range(groups):
                rows = slice(g * blk, (g + 1) * blk)
                near[level, rows, lane(place, blk)] = masked(level * groups + g, level - 1)

    prepare(0)
    turn(0)
    prepare(1)
    pl.semaphore_wait(barrier, nz * nc - 1)

    def load_copy(cut, step):
        to = cols[step]
        levels = pl.ds(cuts[cut][0], cuts[cut][1] - cuts[cut][0])
        return remote(
            turned.at[levels, share(to), :], rhs.at[mine, levels],
            load_s.at[cut, step], load_r.at[cut, mine], (z, to),
        )

    def load_self(cut):
        levels = pl.ds(cuts[cut][0], cuts[cut][1] - cuts[cut][0])
        return pltpu.make_async_copy(
            turned.at[levels, share(c), :], rhs.at[mine, levels], load_own.at[cut]
        )

    def load_start(cut):
        @pl.when(owner)
        def _():
            load_self(cut).start()
            for step in range(1, nc):
                load_copy(cut, step).start()

    def load_wait(cut):
        levels = pl.ds(cuts[cut][0], cuts[cut][1] - cuts[cut][0])
        for g in range(groups):
            @pl.when(trails[g])
            def _():
                here = rhs.at[g, levels]
                remote(
                    here, here, load_s.at[cut, 0], load_r.at[cut, g], (z, sibling)
                ).wait_recv()

        @pl.when(owner)
        def _():
            load_self(cut).wait()

    def diag_copy(level, step):
        to = peers[step]
        return remote(
            split.at[level], diag.at[level, mine],
            diag_s.at[level, step], diag_r.at[level, mine], (z, to),
        )

    def diag_self(level):
        return pltpu.make_async_copy(
            split.at[level], diag.at[level, mine], diag_own.at[level]
        )

    def diag_sib(level):
        here = diag.at[level]
        return remote(here, here, diag_sib_s.at[level], diag_sib_r.at[level], (z, sibling))

    def chip_copy(level, step):
        to = peers[step]
        here = near.at[level, :, lane(place, blk)]
        return remote(here, here, chip_s.at[level, step], chip_r.at[level, step], (z, to))

    def sib_copy(level):
        here = near.at[level, :, lane(core, nc // 2 * blk)]
        return remote(here, here, sib_s.at[level], sib_r.at[level], (z, sibling))

    def spread(level):
        @pl.when(owner)
        def _():
            diag_self(level).start()
            for step in range(1, chips):
                diag_copy(level, step).start()

        if level > 0:
            for step in range(1, chips):
                chip_copy(level, step).start()

    load_start(0)
    spread(0)
    spread(1)
    for level in range(1, LEVELS):
        turn(level)
    load_start(1)
    prepare(2)
    spread(2)
    for level in range(3, LEVELS):
        prepare(level)
    for level in range(2, LEVELS):
        for g in range(groups):
            for col in range(level - 1):
                block = masked(level * groups + g, col)
                own[level, g * blk : (g + 1) * blk, col * blk : (col + 1) * blk] = block

    def relay(level):
        @pl.when(relays)
        def _():
            for g in range(groups):
                @pl.when(leads[g])
                def _():
                    diag_self(level).wait()

                @pl.when(trails[g])
                def _():
                    remote(
                        diag.at[level, g], diag.at[level, g], diag_s.at[level, 0],
                        diag_r.at[level, g], (z, sibling),
                    ).wait_recv()

            diag_sib(level).start()

        if level > 0:
            for step in range(1, chips):
                chip_copy(level, step).wait_recv()
            sib_copy(level).start()

    def arrived(level):
        @pl.when(jnp.logical_not(relays))
        def _():
            diag_sib(level).wait_recv()

        if level > 0:
            sib_copy(level).wait_recv()

    def spread_sent(level):
        @pl.when(owner)
        def _():
            for step in range(1, chips):
                diag_copy(level, step).wait_send()

        @pl.when(relays)
        def _():
            diag_sib(level).wait_send()

        if level > 0:
            for step in range(1, chips):
                chip_copy(level, step).wait_send()
            sib_copy(level).wait_send()

    def y_copy(level, step):
        here = ylow.at[level, :, lane(rank, span)]
        return remote(
            here, here, y_s.at[level, step], y_r.at[level, step], (rows_z[step], c)
        )

    def to_columns(source, dst, s, r, act):
        for g in range(groups):
            src = source(g)

            for step in range(nz):
                def go():
                    copy = remote(
                        src, dst, s.at[step, g], r, (rows_z[step], z + nz * g)
                    )
                    copy.start() if act else copy.wait_send()

                if step > 0:
                    go()
                else:
                    pl.when(trails[g])(go)
                    if act:
                        @pl.when(leads[g])
                        def _():
                            pltpu.make_async_copy(src, dst, r).start()

    def y_far(level, act):
        to_columns(
            lambda g: ylow.at[level, :, lane(rank * groups + g, blk)],
            yfull.at[share(c), pl.ds(level * blk, blk)],
            yf_s.at[level], yf_r.at[level], act,
        )

    batches = {4: LEVELS, 1: 4, 0: 1}

    def out_far(level, act):
        pair = pl.ds(level, batches[level] - level)
        to_columns(
            lambda g: xlow.at[pair, :, pl.ds(g * blk, blk)], landed.at[pair, c],
            out_s.at[level], out_r.at[level], act,
        )

    def f_far(level, act):
        for step in range(1, nc):
            to = cols[step]
            copy = remote(
                fpart.at[level, share(to), :], fsum.at[level, step - 1],
                f_s.at[level, step], f_r.at[level], (z, to),
            )
            copy.start() if act else copy.wait_send()

    def x_far(level, act):
        here = xfull.at[level, share(c), :]
        for step in range(1, nc):
            copy = remote(
                xlow.at[level], here, xf_s.at[level, step], xf_r.at[level], (z, cols[step])
            )
            copy.start() if act else copy.wait_send()
        if act:
            pltpu.make_async_copy(xlow.at[level], here, xf_r.at[level]).start()

    def b_far(level, act):
        for step in range(nc):
            to = cols[step]
            src, dst = bpart.at[level, share(to), :], bsum.at[level, z, :, lane(mine, blk)]

            def go():
                copy = remote(src, dst, b_s.at[level, step], b_r.at[level], (home, to))
                copy.start() if act else copy.wait_send()

            if step > 0:
                go()
            else:
                pl.when(jnp.logical_not(owner))(go)
                if act:
                    @pl.when(owner)
                    def _():
                        pltpu.make_async_copy(src, dst, b_r.at[level]).start()

    def all_in(ref, sem):
        pltpu.make_async_copy(ref, ref, sem).wait()

    def apply(value, low, rest, dims):
        axis = dims[0][1][0]
        high, small = halves(value)
        left = jnp.concatenate([high, small, high], axis=1)
        return dot(left, jnp.concatenate([low, low, rest], axis=axis), dims)

    def solve(level, value, dims):
        return [
            apply(
                value[:, g * blk : (g + 1) * blk],
                diag[level, g, :, :blk], diag[level, g, :, blk:], dims,
            )
            for g in range(groups)
        ]

    relay(0)
    load_wait(0)

    for level in range(LEVELS):
        for cut in range(1, len(cuts)):
            if level == cuts[cut][0]:
                load_wait(cut)
        arrived(level)
        resid = jnp.concatenate([rhs[g, level] for g in range(groups)], axis=1)
        if level > 0:
            for step in range(1, nz):
                y_copy(level - 1, step).wait_recv()
            resid = resid - dot(ylow[level - 1], near[level], NT)
        if level > 1:
            resid = resid - fpart[level, share(c), :].astype(jnp.float32)
            all_in(fsum.at[level], f_r.at[level])
            for step in range(nc - 1):
                resid = resid - fsum[level, step].astype(jnp.float32)
        solved = jnp.concatenate(solve(level, resid, NT), axis=1)
        yval[level] = solved
        if level < last:
            ylow[level, :, lane(rank, span)] = solved.astype(jnp.bfloat16)
            for step in range(1, nz):
                y_copy(level, step).start()
            if level < last - 1:
                y_far(level, True)
            if level > 0:
                value = None
                if level > 1:
                    done = slice(0, (level - 1) * blk)
                    value = dot(yfull[:, done], own[level + 1, :, done], NT)
                fresh = slice((level - 1) * blk, level * blk)
                all_in(yfull.at[:, pl.ds((level - 1) * blk, blk)], yf_r.at[level - 1])
                term = dot(yfull[:, fresh], own[level + 1, :, fresh], NT)
                value = term if value is None else value + term
                fpart[level + 1] = value.astype(jnp.bfloat16)
                f_far(level + 1, True)
            if level + 3 < LEVELS:
                spread(level + 3)
            if level == 0:
                load_start(2)
            relay(level + 1)

    def part_copy(level, step):
        return remote(
            part.at[level, :, lane(ranks[step], span)], sums.at[level, step - 1],
            p_s.at[level, step], p_r.at[level, step], (rows_z[step], c),
        )

    for level in reversed(range(LEVELS)):
        if level < last:
            value = dot(xlow[level + 1], near[level + 1], NN)
            part[level] = value.astype(jnp.bfloat16)
            for step in range(1, nz):
                part_copy(level, step).start()
            if level > 0:
                x_far(level + 1, True)
                value = None
                lanes = slice((level - 1) * blk, level * blk)
                for up in reversed(range(level + 1, LEVELS)):
                    if up == level + 1:
                        all_in(xfull.at[up], xf_r.at[up])
                    term = dot(xfull[up], own[up, :, lanes], NN)
                    value = term if value is None else value + term
                bpart[level - 1] = value.astype(jnp.bfloat16)
                b_far(level - 1, True)
            if level + 1 in batches:
                out_far(level + 1, True)
        resid = yval[level]
        if level < last:
            resid = resid - part[level, :, lane(rank, span)].astype(jnp.float32)
        if level < last - 1:
            all_in(bsum.at[level], b_r.at[level])
            for step in range(nz):
                resid = resid - bsum[level, step].astype(jnp.float32)
        if level < last:
            for step in range(1, nz):
                part_copy(level, step).wait_recv()
                resid = resid - sums[level, step - 1].astype(jnp.float32)
        solved = jnp.concatenate(solve(level, resid, NN), axis=1)
        xlow[level] = solved.astype(jnp.bfloat16)

    out_far(0, True)
    for level in range(last):
        for step in range(1, nz):
            y_copy(level, step).wait_send()
            part_copy(level, step).wait_send()
        if level < last - 1:
            y_far(level, False)
            b_far(level, False)
            f_far(level + 2, False)
            x_far(level + 2, False)
    for level in range(LEVELS):
        spread_sent(level)

    @pl.when(owner)
    def _():
        for cut in range(len(cuts)):
            for step in range(1, nc):
                load_copy(cut, step).wait_send()

    for level, stop in batches.items():
        out_far(level, False)
        all_in(landed.at[pl.ds(level, stop - level)], out_r.at[level])
        out[level:stop] = landed[level:stop]


def split_plan(factor, pattern, loads, block_inverse):
    nz, nc = lax.axis_size("row"), lax.axis_size("col")
    rows, cols, blk = factor.shape[0], factor.shape[2], factor.shape[4]
    scen = loads.shape[3]
    groups, chips, width = nc // nz, nc // 2, scen // nc
    span = groups * blk
    low, f32 = jnp.bfloat16, jnp.float32
    dma = pltpu.SemaphoreType.DMA
    vmem = pl.BlockSpec(memory_space=pltpu.VMEM)
    smem = pl.BlockSpec(memory_space=pltpu.SMEM)
    result = pl.pallas_call(
        functools.partial(kernel, nz, nc, blk, scen),
        out_shape=jax.ShapeDtypeStruct((LEVELS, nc, width, blk), low),
        in_specs=[vmem, smem, vmem, vmem],
        out_specs=vmem,
        scratch_shapes=[
            pltpu.VMEM((LEVELS, scen, blk), f32),
            pltpu.VMEM((LEVELS, blk, 2 * blk), low),
            pltpu.VMEM((LEVELS, span, nc * blk), low),
            pltpu.VMEM((LEVELS, span, cols * blk), low),
            pltpu.VMEM((groups, LEVELS, width, blk), f32),
            pltpu.VMEM((LEVELS, groups, blk, 2 * blk), low),
            pltpu.VMEM((LEVELS, width, span), f32),
            pltpu.VMEM((LEVELS, width, nc * blk), low),
            pltpu.VMEM((scen, LEVELS * blk), low),
            pltpu.VMEM((LEVELS, scen, span), low),
            pltpu.VMEM((LEVELS, nc - 1, width, span), low),
            pltpu.VMEM((LEVELS, width, span), low),
            pltpu.VMEM((LEVELS, scen, span), low),
            pltpu.VMEM((LEVELS, width, nc * blk), low),
            pltpu.VMEM((LEVELS, nz - 1, width, span), low),
            pltpu.VMEM((LEVELS, scen, blk), low),
            pltpu.VMEM((LEVELS, nz, width, span), low),
            pltpu.VMEM((LEVELS, nc, width, blk), low),
            dma((LEVELS,)), dma((LEVELS,)),
            dma((LEVELS, chips)), dma((LEVELS, chips)),
            dma((3,)), dma((3, nc)), dma((3, groups)),
            dma((LEVELS,)), dma((LEVELS, chips)), dma((LEVELS, groups)),
            dma((LEVELS,)), dma((LEVELS,)),
            dma((LEVELS, nz)), dma((LEVELS, nz)),
            dma((LEVELS, nz, groups)), dma((LEVELS,)),
            dma((LEVELS, nc)), dma((LEVELS,)),
            dma((LEVELS, nz)), dma((LEVELS, nz)),
            dma((LEVELS, nc)), dma((LEVELS,)),
            dma((LEVELS, nc)), dma((LEVELS,)),
            dma((LEVELS, nz, groups)), dma((LEVELS,)),
        ],
        compiler_params=pltpu.CompilerParams(
            collective_id=0, has_side_effects=True, vmem_limit_bytes=52 * 2**20
        ),
    )(factor[:, 0, :, 0], pattern[:, 0, :, 0], loads[:, 0], block_inverse[:, 0])
    result = result.reshape(LEVELS, scen, blk).astype(f32)
    return jnp.swapaxes(result, 1, 2)[:, None]


def pick_plan(mesh):
    def plan(factor, pattern, loads, block_inverse):
        nz, nc = mesh.shape["row"], mesh.shape["col"]
        scen = loads.shape[3]
        small = nc * factor.size * 2 <= 32 * 2**20
        single = factor.shape[2] == LEVELS and factor.shape[0] == LEVELS * (nc // nz)
        even = nc % nz == 0 and nc % 2 == 0 and nz % 2 == 0 and scen % (16 * nc) == 0
        if small and even and single and loads.shape[0] == LEVELS:
            return split_plan(factor, pattern, loads, block_inverse)
        return per_device(factor, pattern, loads, block_inverse)

    return plan


def solution(mesh):
    in_specs = (
        P(None, "row", None, "col", None, None),
        P(None, "row", None, "col"),
        P(None, "col", None, None),
        P(None, "col", None, None),
    )
    out_specs = P(None, "col", None, None)
    return jax.shard_map(
        pick_plan(mesh), mesh=mesh, in_specs=in_specs, out_specs=out_specs, check_vma=False
    )
```

```python
import functools

import jax
import jax.numpy as jnp
from jax import lax
from jax.experimental import pallas as pl
from jax.experimental.pallas import tpu as pltpu
from jax.sharding import PartitionSpec as P

LEVELS = 8


def spread(value, axis, source):
    kept = jnp.where(lax.axis_index(axis) == source, value, 0).astype(value.dtype)
    return lax.psum(kept, axis)


def per_device(factor, pattern, loads, block_inverse):
    row_count = lax.axis_size("row")
    col_count = lax.axis_size("col")
    groups = col_count // row_count
    my_row = lax.axis_index("row")
    my_col = lax.axis_index("col")
    masked = factor[:, 0, :, 0] * pattern[:, 0, :, 0].astype(jnp.bfloat16)[:, :, None, None]
    per_row = factor.shape[0] // LEVELS
    per_col = factor.shape[2] // LEVELS
    rhs_local = loads[:, 0]
    inverse_local = block_inverse[:, 0]
    forward_vals = []
    forward_low = []
    for level_id in range(LEVELS):
        rhs_level = rhs_local[level_id * per_col : (level_id + 1) * per_col]
        inverse_level = inverse_local[level_id * per_col : (level_id + 1) * per_col]
        if level_id > 0:
            panel = masked[level_id * per_row : (level_id + 1) * per_row, : level_id * per_col]
            earlier = jnp.concatenate(forward_low, axis=0)
            partial_sum = jnp.einsum(
                "abpq,bqs->aps", panel, earlier, preferred_element_type=jnp.float32
            )
            row_total = lax.psum(partial_sum, "col")
            row_total = row_total.reshape((per_col, groups) + row_total.shape[1:])
            own_total = lax.dynamic_index_in_dim(
                row_total, my_col // row_count, axis=1, keepdims=False
            )
            solved = jnp.einsum(
                "mpq,mqs->mps",
                inverse_level,
                rhs_level - own_total,
                precision=lax.Precision.HIGHEST,
            )
            solved = spread(solved, "row", my_col % row_count)
        else:
            solved = jnp.einsum(
                "mpq,mqs->mps", inverse_level, rhs_level, precision=lax.Precision.HIGHEST
            )
        forward_vals.append(solved)
        forward_low.append(solved.astype(jnp.bfloat16))
    solution_parts = [None] * LEVELS
    later = []
    for level_id in reversed(range(LEVELS)):
        inverse_level = inverse_local[level_id * per_col : (level_id + 1) * per_col]
        resid = forward_vals[level_id]
        if level_id < LEVELS - 1:
            panel = masked[
                (level_id + 1) * per_row :, level_id * per_col : (level_id + 1) * per_col
            ]
            after = jnp.concatenate(later, axis=0)
            partial_sum = jnp.einsum(
                "abpq,aps->bqs", panel, after, preferred_element_type=jnp.float32
            )
            resid = resid - lax.psum(partial_sum, "row")
        solved = jnp.einsum("mqp,mqs->mps", inverse_level, resid, precision=lax.Precision.HIGHEST)
        solution_parts[level_id] = solved
        if level_id > 0:
            low_solved = solved.astype(jnp.bfloat16)
            pieces = lax.all_gather(low_solved[None], "col", axis=0, tiled=True)
            pieces = pieces.reshape((groups, row_count) + low_solved.shape)
            picked = lax.dynamic_index_in_dim(pieces, my_row, axis=1, keepdims=False)
            arranged = jnp.swapaxes(picked, 0, 1).reshape((per_row,) + low_solved.shape[1:])
            later = [arranged] + later
    solution = jnp.concatenate(solution_parts, axis=0)
    return solution[:, None]


MESH = pl.DeviceIdType.MESH
NT = (((1,), (1,)), ((), ()))
NN = (((1,), (0,)), ((), ()))


def dot(a, b, dims):
    return lax.dot_general(a, b, dims, preferred_element_type=jnp.float32)


def kernel(
    nz, nc, blk, scen, factor, pattern, loads, inverse, out,
    turned, split, near, own, rhs, diag, yval, ylow, yfull, fpart, fsum, xlow, xfull,
    part, sums, bpart, bsum, landed,
    sib_s, sib_r, chip_s, chip_r,
    load_own, load_s, load_r, diag_own, diag_s, diag_r, diag_sib_s, diag_sib_r,
    y_s, y_r, yf_s, yf_r, f_s, f_r, p_s, p_r, xf_s, xf_r, b_s, b_r, out_s, out_r,
):
    groups = nc // nz
    chips = nc // 2
    width = scen // nc
    last = LEVELS - 1
    z = lax.axis_index("row")
    c = lax.axis_index("col")
    chip = c // 2
    core = c % 2
    sibling = chip * 2 + 1 - core
    owner = c % nz == z
    leads = [c == z + nz * g for g in range(nc // nz)]
    trails = [c != z + nz * g for g in range(nc // nz)]
    relays = core == z % 2
    mine = c // nz
    span = groups * blk
    rank = (z % 2) * (nz // 2) + z // 2
    cols = [c] + [(c + step) % nc for step in range(1, nc)]
    rows_z = [z] + [(z + step) % nz for step in range(1, nz)]
    ranks = [rank] + [(to % 2) * (nz // 2) + to // 2 for to in rows_z[1:]]
    peers = [c] + [((chip + step) % chips) * 2 + core for step in range(1, chips)]
    home = c % nz
    place = ((home % 2) * (nz // 2) + home // 2) * groups + mine
    cuts = ((0, 1), (1, 3), (3, LEVELS))

    barrier = pltpu.get_barrier_semaphore()
    for step in range(1, nz * nc):
        other = (z * nc + c + step) % (nz * nc)
        pl.semaphore_signal(
            barrier, inc=1, device_id=(other // nc, other % nc), device_id_type=MESH
        )

    def remote(src, dst, s, r, to):
        return pltpu.make_async_remote_copy(
            src_ref=src, dst_ref=dst, send_sem=s, recv_sem=r, device_id=to, device_id_type=MESH
        )

    def share(col):
        return pl.ds(pl.multiple_of(col * width, width), width)

    def masked(row, col):
        return factor[row, col] * pattern[row, col].astype(jnp.float32).astype(jnp.bfloat16)

    def lane(index, size):
        return pl.ds(pl.multiple_of(index * size, size), size)

    def turn(level):
        turned[level] = loads[level].T

    def halves(value):
        high = value.astype(jnp.bfloat16)
        return high, (value - high.astype(jnp.float32)).astype(jnp.bfloat16)

    def prepare(level):
        high, rest = halves(inverse[level])
        split[level, :, :blk] = high
        split[level, :, blk:] = rest
        if level > 0:
            for g in range(groups):
                rows = slice(g * blk, (g + 1) * blk)
                near[level, rows, lane(place, blk)] = masked(level * groups + g, level - 1)

    prepare(0)
    turn(0)
    prepare(1)
    pl.semaphore_wait(barrier, nz * nc - 1)

    def load_copy(cut, step):
        to = cols[step]
        levels = pl.ds(cuts[cut][0], cuts[cut][1] - cuts[cut][0])
        return remote(
            turned.at[levels, share(to), :], rhs.at[mine, levels],
            load_s.at[cut, step], load_r.at[cut, mine], (z, to),
        )

    def load_self(cut):
        levels = pl.ds(cuts[cut][0], cuts[cut][1] - cuts[cut][0])
        return pltpu.make_async_copy(
            turned.at[levels, share(c), :], rhs.at[mine, levels], load_own.at[cut]
        )

    def load_start(cut):
        @pl.when(owner)
        def _():
            load_self(cut).start()
            for step in range(1, nc):
                load_copy(cut, step).start()

    def load_wait(cut):
        levels = pl.ds(cuts[cut][0], cuts[cut][1] - cuts[cut][0])
        for g in range(groups):
            @pl.when(trails[g])
            def _():
                here = rhs.at[g, levels]
                remote(
                    here, here, load_s.at[cut, 0], load_r.at[cut, g], (z, sibling)
                ).wait_recv()

        @pl.when(owner)
        def _():
            load_self(cut).wait()

    def diag_copy(level, step):
        to = peers[step]
        return remote(
            split.at[level], diag.at[level, mine],
            diag_s.at[level, step], diag_r.at[level, mine], (z, to),
        )

    def diag_self(level):
        return pltpu.make_async_copy(
            split.at[level], diag.at[level, mine], diag_own.at[level]
        )

    def diag_sib(level):
        here = diag.at[level]
        return remote(here, here, diag_sib_s.at[level], diag_sib_r.at[level], (z, sibling))

    def chip_copy(level, step):
        to = peers[step]
        here = near.at[level, :, lane(place, blk)]
        return remote(here, here, chip_s.at[level, step], chip_r.at[level, step], (z, to))

    def sib_copy(level):
        here = near.at[level, :, lane(core, nc // 2 * blk)]
        return remote(here, here, sib_s.at[level], sib_r.at[level], (z, sibling))

    def spread(level):
        @pl.when(owner)
        def _():
            diag_self(level).start()
            for step in range(1, chips):
                diag_copy(level, step).start()

        if level > 0:
            for step in range(1, chips):
                chip_copy(level, step).start()

    load_start(0)
    spread(0)
    spread(1)
    for level in range(1, LEVELS):
        turn(level)
    load_start(1)
    prepare(2)
    spread(2)
    for level in range(3, LEVELS):
        prepare(level)
    for level in range(2, LEVELS):
        for g in range(groups):
            for col in range(level - 1):
                block = masked(level * groups + g, col)
                own[level, g * blk : (g + 1) * blk, col * blk : (col + 1) * blk] = block

    def relay(level):
        @pl.when(relays)
        def _():
            for g in range(groups):
                @pl.when(leads[g])
                def _():
                    diag_self(level).wait()

                @pl.when(trails[g])
                def _():
                    remote(
                        diag.at[level, g], diag.at[level, g], diag_s.at[level, 0],
                        diag_r.at[level, g], (z, sibling),
                    ).wait_recv()

            diag_sib(level).start()

        if level > 0:
            for step in range(1, chips):
                chip_copy(level, step).wait_recv()
            sib_copy(level).start()

    def arrived(level):
        @pl.when(jnp.logical_not(relays))
        def _():
            diag_sib(level).wait_recv()

        if level > 0:
            sib_copy(level).wait_recv()

    def spread_sent(level):
        @pl.when(owner)
        def _():
            for step in range(1, chips):
                diag_copy(level, step).wait_send()

        @pl.when(relays)
        def _():
            diag_sib(level).wait_send()

        if level > 0:
            for step in range(1, chips):
                chip_copy(level, step).wait_send()
            sib_copy(level).wait_send()

    def y_copy(level, step):
        here = ylow.at[level, :, lane(rank, span)]
        return remote(
            here, here, y_s.at[level], y_r.at[level, step], (rows_z[step], c)
        )

    def to_columns(source, dst, s, r, act, single):
        for g in range(groups):
            src = source(g)

            for step in range(nz):
                def go():
                    copy = remote(
                        src, dst, s if single else s.at[step, g], r, (rows_z[step], z + nz * g)
                    )
                    copy.start() if act else copy.wait_send()

                if step > 0:
                    go()
                else:
                    pl.when(trails[g])(go)
                    if act:
                        @pl.when(leads[g])
                        def _():
                            pltpu.make_async_copy(src, dst, r).start()

    def y_far(level, act):
        to_columns(
            lambda g: ylow.at[level, :, lane(rank * groups + g, blk)],
            yfull.at[share(c), pl.ds(level * blk, blk)],
            yf_s.at[level], yf_r.at[level], act, True,
        )

    batches = {4: LEVELS, 1: 4, 0: 1}

    def out_far(level, act):
        pair = pl.ds(level, batches[level] - level)
        to_columns(
            lambda g: xlow.at[pair, :, pl.ds(g * blk, blk)], landed.at[pair, c],
            out_s.at[level], out_r.at[level], act, False,
        )

    def f_far(level, act):
        for step in range(1, nc):
            to = cols[step]
            copy = remote(
                fpart.at[level, share(to), :], fsum.at[level, step - 1],
                f_s.at[level], f_r.at[level], (z, to),
            )
            copy.start() if act else copy.wait_send()

    def x_far(level, act):
        here = xfull.at[level, share(c), :]
        for step in range(1, nc):
            copy = remote(
                xlow.at[level], here, xf_s.at[level], xf_r.at[level], (z, cols[step])
            )
            copy.start() if act else copy.wait_send()
        if act:
            pltpu.make_async_copy(xlow.at[level], here, xf_r.at[level]).start()

    def b_far(level, act):
        for step in range(nc):
            to = cols[step]
            src, dst = bpart.at[level, share(to), :], bsum.at[level, z, :, lane(mine, blk)]

            def go():
                copy = remote(src, dst, b_s.at[level], b_r.at[level], (home, to))
                copy.start() if act else copy.wait_send()

            if step > 0:
                go()
            else:
                pl.when(jnp.logical_not(owner))(go)
                if act:
                    @pl.when(owner)
                    def _():
                        pltpu.make_async_copy(src, dst, b_r.at[level]).start()

    def all_in(ref, sem):
        pltpu.make_async_copy(ref, ref, sem).wait()

    def apply(value, low, rest, dims):
        axis = dims[0][1][0]
        high, small = halves(value)
        left = jnp.concatenate([high, small, high], axis=1)
        return dot(left, jnp.concatenate([low, low, rest], axis=axis), dims)

    def solve(level, value, dims):
        return [
            apply(
                value[:, g * blk : (g + 1) * blk],
                diag[level, g, :, :blk], diag[level, g, :, blk:], dims,
            )
            for g in range(groups)
        ]

    relay(0)
    load_wait(0)

    for level in range(LEVELS):
        for cut in range(1, len(cuts)):
            if level == cuts[cut][0]:
                load_wait(cut)
        arrived(level)
        resid = jnp.concatenate([rhs[g, level] for g in range(groups)], axis=1)
        if level > 0:
            for step in range(1, nz):
                y_copy(level - 1, step).wait_recv()
            resid = resid - dot(ylow[level - 1], near[level], NT)
        if level > 1:
            resid = resid - fpart[level, share(c), :].astype(jnp.float32)
            all_in(fsum.at[level], f_r.at[level])
            for step in range(nc - 1):
                resid = resid - fsum[level, step].astype(jnp.float32)
        solved = jnp.concatenate(solve(level, resid, NT), axis=1)
        yval[level] = solved
        if level < last:
            ylow[level, :, lane(rank, span)] = solved.astype(jnp.bfloat16)
            for step in range(1, nz):
                y_copy(level, step).start()
            if level < last - 1:
                y_far(level, True)
            if level > 0:
                value = None
                if level > 1:
                    done = slice(0, (level - 1) * blk)
                    value = dot(yfull[:, done], own[level + 1, :, done], NT)
                fresh = slice((level - 1) * blk, level * blk)
                all_in(yfull.at[:, pl.ds((level - 1) * blk, blk)], yf_r.at[level - 1])
                term = dot(yfull[:, fresh], own[level + 1, :, fresh], NT)
                value = term if value is None else value + term
                fpart[level + 1] = value.astype(jnp.bfloat16)
                f_far(level + 1, True)
            if level + 3 < LEVELS:
                spread(level + 3)
            if level == 0:
                load_start(2)
            relay(level + 1)

    def part_copy(level, step):
        return remote(
            part.at[level, :, lane(ranks[step], span)], sums.at[level, step - 1],
            p_s.at[level], p_r.at[level, step], (rows_z[step], c),
        )

    for level in reversed(range(LEVELS)):
        if level < last:
            value = dot(xlow[level + 1], near[level + 1], NN)
            part[level] = value.astype(jnp.bfloat16)
            for step in range(1, nz):
                part_copy(level, step).start()
            if level > 0:
                x_far(level + 1, True)
                value = None
                lanes = slice((level - 1) * blk, level * blk)
                for up in reversed(range(level + 1, LEVELS)):
                    if up == level + 1:
                        all_in(xfull.at[up], xf_r.at[up])
                    term = dot(xfull[up], own[up, :, lanes], NN)
                    value = term if value is None else value + term
                bpart[level - 1] = value.astype(jnp.bfloat16)
                b_far(level - 1, True)
            if level + 1 in batches:
                out_far(level + 1, True)
        resid = yval[level]
        if level < last:
            resid = resid - part[level, :, lane(rank, span)].astype(jnp.float32)
        if level < last - 1:
            all_in(bsum.at[level], b_r.at[level])
            for step in range(nz):
                resid = resid - bsum[level, step].astype(jnp.float32)
        if level < last:
            for step in range(1, nz):
                part_copy(level, step).wait_recv()
                resid = resid - sums[level, step - 1].astype(jnp.float32)
        solved = jnp.concatenate(solve(level, resid, NN), axis=1)
        xlow[level] = solved.astype(jnp.bfloat16)

    out_far(0, True)
    for level in range(last):
        all_in(sums.at[level], y_s.at[level])
        all_in(sums.at[level], p_s.at[level])
        if level < last - 1:
            all_in(fsum.at[level + 2], f_s.at[level + 2])
            all_in(fsum.at[level + 2], xf_s.at[level + 2])

    @pl.when(owner)
    def _():
        for level in range(last - 1):
            all_in(landed.at[level, pl.ds(0, nc - 1)], yf_s.at[level])
            all_in(landed.at[level, pl.ds(0, nc - 1)], b_s.at[level])

    @pl.when(jnp.logical_not(owner))
    def _():
        for level in range(last - 1):
            all_in(landed.at[level], yf_s.at[level])
            all_in(landed.at[level], b_s.at[level])

    for level in range(LEVELS):
        spread_sent(level)

    @pl.when(owner)
    def _():
        for cut in range(len(cuts)):
            for step in range(1, nc):
                load_copy(cut, step).wait_send()

    for level, stop in batches.items():
        out_far(level, False)
        all_in(landed.at[pl.ds(level, stop - level)], out_r.at[level])
        out[level:stop] = landed[level:stop]


def split_plan(factor, pattern, loads, block_inverse):
    nz, nc = lax.axis_size("row"), lax.axis_size("col")
    rows, cols, blk = factor.shape[0], factor.shape[2], factor.shape[4]
    scen = loads.shape[3]
    groups, chips, width = nc // nz, nc // 2, scen // nc
    span = groups * blk
    low, f32 = jnp.bfloat16, jnp.float32
    dma = pltpu.SemaphoreType.DMA
    vmem = pl.BlockSpec(memory_space=pltpu.VMEM)
    smem = pl.BlockSpec(memory_space=pltpu.SMEM)
    result = pl.pallas_call(
        functools.partial(kernel, nz, nc, blk, scen),
        out_shape=jax.ShapeDtypeStruct((LEVELS, nc, width, blk), low),
        in_specs=[vmem, smem, vmem, vmem],
        out_specs=vmem,
        scratch_shapes=[
            pltpu.VMEM((LEVELS, scen, blk), f32),
            pltpu.VMEM((LEVELS, blk, 2 * blk), low),
            pltpu.VMEM((LEVELS, span, nc * blk), low),
            pltpu.VMEM((LEVELS, span, cols * blk), low),
            pltpu.VMEM((groups, LEVELS, width, blk), f32),
            pltpu.VMEM((LEVELS, groups, blk, 2 * blk), low),
            pltpu.VMEM((LEVELS, width, span), f32),
            pltpu.VMEM((LEVELS, width, nc * blk), low),
            pltpu.VMEM((scen, LEVELS * blk), low),
            pltpu.VMEM((LEVELS, scen, span), low),
            pltpu.VMEM((LEVELS, nc - 1, width, span), low),
            pltpu.VMEM((LEVELS, width, span), low),
            pltpu.VMEM((LEVELS, scen, span), low),
            pltpu.VMEM((LEVELS, width, nc * blk), low),
            pltpu.VMEM((LEVELS, nz - 1, width, span), low),
            pltpu.VMEM((LEVELS, scen, blk), low),
            pltpu.VMEM((LEVELS, nz, width, span), low),
            pltpu.VMEM((LEVELS, nc, width, blk), low),
            dma((LEVELS,)), dma((LEVELS,)),
            dma((LEVELS, chips)), dma((LEVELS, chips)),
            dma((3,)), dma((3, nc)), dma((3, groups)),
            dma((LEVELS,)), dma((LEVELS, chips)), dma((LEVELS, groups)),
            dma((LEVELS,)), dma((LEVELS,)),
            dma((LEVELS,)), dma((LEVELS, nz)),
            dma((LEVELS,)), dma((LEVELS,)),
            dma((LEVELS,)), dma((LEVELS,)),
            dma((LEVELS,)), dma((LEVELS, nz)),
            dma((LEVELS,)), dma((LEVELS,)),
            dma((LEVELS,)), dma((LEVELS,)),
            dma((LEVELS, nz, groups)), dma((LEVELS,)),
        ],
        compiler_params=pltpu.CompilerParams(
            collective_id=0, has_side_effects=True, vmem_limit_bytes=52 * 2**20
        ),
    )(factor[:, 0, :, 0], pattern[:, 0, :, 0], loads[:, 0], block_inverse[:, 0])
    result = result.reshape(LEVELS, scen, blk).astype(f32)
    return jnp.swapaxes(result, 1, 2)[:, None]


def pick_plan(mesh):
    def plan(factor, pattern, loads, block_inverse):
        nz, nc = mesh.shape["row"], mesh.shape["col"]
        scen = loads.shape[3]
        small = nc * factor.size * 2 <= 32 * 2**20
        single = factor.shape[2] == LEVELS and factor.shape[0] == LEVELS * (nc // nz)
        even = nc % nz == 0 and nc % 2 == 0 and nz % 2 == 0 and scen % (16 * nc) == 0
        if small and even and single and loads.shape[0] == LEVELS:
            return split_plan(factor, pattern, loads, block_inverse)
        return per_device(factor, pattern, loads, block_inverse)

    return plan


def solution(mesh):
    in_specs = (
        P(None, "row", None, "col", None, None),
        P(None, "row", None, "col"),
        P(None, "col", None, None),
        P(None, "col", None, None),
    )
    out_specs = P(None, "col", None, None)
    return jax.shard_map(
        pick_plan(mesh), mesh=mesh, in_specs=in_specs, out_specs=out_specs, check_vma=False
    )
```
